256 devices in a mesh: section: 4 (over y), ctx: 8 (over z), exp: 8 (over x, core).
Axes of the slice: x: 4, y: 4, z: 8, core: 2. Of those that a mesh axis runs over, the one named last changes fastest.
Arguments:
- hidden_in: bfloat16 [4, 8, 1024, 4096], P('section', 'exp', 'ctx'), may hold values from -6 to 6
- queries: bfloat16 [4, 8, 1024, 4096], P('section', 'exp', 'ctx'), may hold values from -6 to 6
- keys: bfloat16 [4, 8, 1024, 256], P('section', 'exp', 'ctx'), may hold values from -6 to 6
- values: bfloat16 [4, 8, 1024, 256], P('section', 'exp', 'ctx'), may hold values from -6 to 6
- out_weight: bfloat16 [4, 4096, 4096], P('section', 'ctx'), may hold values from -0.5 to 0.5
- norm_gain: bfloat16 [4, 4096], P('section'), may hold values from 0.5 to 1.5
- w_gate: bfloat16 [4, 8, 4096, 1536], P('section', 'exp', None, 'ctx'), may hold values from -0.09375 to 0.09375
- w_up: bfloat16 [4, 8, 4096, 1536], P('section', 'exp', None, 'ctx'), may hold values from -0.09375 to 0.09375
- w_down_t: bfloat16 [4, 8, 4096, 1536], P('section', 'exp', None, 'ctx'), may hold values from -0.15625 to 0.15625
- expert_ids: int32 [4, 8, 1024, 1], P('section', 'exp', 'ctx'), may hold values from 0 to 7; in each aligned block of 128 rows (0 to 127, 128 to 255, ..., all dimensions but the last counted through in order) at most 20 rows name the same one
- route_gates: float32 [4, 8, 1024, 1], P('section', 'exp', 'ctx'), may hold values from 0.1 to 1
Outputs:
- next_input: bfloat16 [4, 8, 1024, 4096], P('section', 'exp', 'ctx')
The draws below stay inside these ranges and needn't reach their ends.
Inputs may be any that keep to these rules, and one draw needn't show every extreme that they name: `expert_ids`: within the rows of one device (aligned blocks of 128 positions of a sequence, routes taken together), no expert is named by more than 20 routes.
All inputs are finite; a program needn't handle non-finite values.
Results may differ from the reference program's by a relative error of at most 0.018.
Values may be sent and summed in bfloat16 or wider, within the bound.
A program may use at most 128 MiB of HBM per device.

```python
import math
import jax
import jax.numpy as jnp
import numpy as np
from jax import lax

D = 4096
QUERY_HEADS = 32
KEY_VALUE_HEADS = 2
HEAD_SIZE = 128
FF = 1536
TOP = 1
TOK_DEV = 128
EXPERTS = 8
SEQUENCE_LENGTH = 1024
CAP = 20
N_SECTION = 4
N_CTX = 8
N_EXP = 8


def draw_keys(key, part):
    key = jax.random.fold_in(key, 5)
    sampled_values = jnp.clip(jax.random.normal(key, (N_SECTION, N_EXP, SEQUENCE_LENGTH, KEY_VALUE_HEADS, HEAD_SIZE), jnp.float32), -6.0, 6.0)
    return sampled_values.reshape(N_SECTION, N_EXP, SEQUENCE_LENGTH, KEY_VALUE_HEADS * HEAD_SIZE).astype(jnp.bfloat16)


def draw_queries(key, part):
    key = jax.random.fold_in(key, 6)
    sampled_values = jnp.clip(jax.random.normal(key, (N_SECTION, N_EXP, SEQUENCE_LENGTH, QUERY_HEADS, HEAD_SIZE), jnp.float32), -6.0, 6.0)
    return sampled_values.reshape(N_SECTION, N_EXP, SEQUENCE_LENGTH, QUERY_HEADS * HEAD_SIZE).astype(jnp.bfloat16)


def block_levels(stream_key, dims, split, least, largest):
    loudness, own = 1.0, jax.random.fold_in(stream_key, 6)
    for dim, blocks in split:
        steps = jnp.exp(jax.random.uniform(jax.random.fold_in(own, dim), (blocks,), jnp.float32, least / len(split), largest / len(split)))
        loudness = loudness * jnp.repeat(steps, dims[dim] // blocks).reshape([-1 if axis == dim else 1 for axis in range(len(dims))])
    return loudness


def routed_block(own_key, own, number, rows, count, top, most, lean):
    order = jax.random.permutation(own_key, count)
    heavy_load, usual = portions_of(count, rows * top, most, lean, True), portions_of(count, rows * top, most, lean, False)
    places = jnp.arange(count)

    def named(tallies, offset_by):
        used = int((tallies > 0).sum())
        fixed = max(1, used // 4)
        passed = fixed + (places - fixed + offset_by * (used - fixed)) % max(1, count - fixed)
        return jnp.zeros((count,), jnp.int32).at[order[jnp.where(places < fixed, places, passed)]].set(jnp.asarray(tallies, jnp.int32))

    tallies = jnp.where(number % 4 == 0, named(heavy_load, number // 4), named(usual, number - number // 4 - 1))
    mixed = jax.random.permutation(jax.random.fold_in(own, 3), count)
    source_of, receiver = mixed[0:count // 2 * 2:2], mixed[1:count // 2 * 2:2]
    room = jnp.minimum(tallies[source_of] - 1, most - tallies[receiver]) // 2
    room = jnp.where((source_of == order[0]) | (receiver == order[0]) | (tallies[receiver] == 0), 0, jnp.maximum(room, 0))
    passed = jax.random.randint(jax.random.fold_in(own, 4), (count // 2,), 0, 1 << 20) % (room + 1)
    tallies = tallies.at[source_of].add(-passed).at[receiver].add(passed)
    items = jnp.searchsorted(jnp.cumsum(tallies), jnp.arange(rows * top), side="right").astype(jnp.int32)
    table = items.reshape(top, rows).T
    table = table[jax.random.permutation(jax.random.fold_in(own, 1), rows)]
    offset_by = jax.random.randint(jax.random.fold_in(own, 2), (rows, 1), 0, top)
    return jnp.take_along_axis(table, (jnp.arange(top)[None, :] + offset_by) % top, axis=1)


def portions_of(count, total, limit, slope, full):
    weights = [(1 << 20) // math.isqrt(standing ** slope) + 1 for standing in range(1, count + 1)]
    largest = limit if full else min(limit, max(-(-total // count), total * weights[0] // sum(weights)))
    least = 1 if total - largest >= count - 1 else 0
    holding, rest = [largest] + [least] * (count - 1), total - largest - least * (count - 1)
    while rest > 0:
        movable = [i for i in range(1, count) if holding[i] < largest] or [i for i in range(1, count) if holding[i] < limit]
        whole, left = sum([weights[i] for i in movable]), rest
        for i in movable:
            more = min(limit - holding[i], max(1, left * weights[i] // whole), rest)
            holding[i] = holding[i] + more
            rest = rest - more
    return np.array(holding)


def centred(own_key, shape, width, limit, cuts=(), held_as=jnp.bfloat16):
    result = width * jax.random.normal(own_key, shape, jnp.float32)
    if cuts:
        result = result * block_levels(own_key, shape, cuts, -0.22, 0.18)
    return jnp.clip(result, -limit, limit).astype(held_as)


def setup_inputs(seed: int = 0) -> dict:
    key_list = jax.random.split(jax.random.key(seed), 12)
    hidden_in = centred(key_list[0], (N_SECTION, N_EXP, SEQUENCE_LENGTH, D), 1.0, 6.0, ((0, 4), (1, 8), (2, 8)))
    queries = draw_queries(jax.random.fold_in(key_list[11], 71), 0)
    keys = draw_keys(jax.random.fold_in(key_list[11], 71), 0)
    values = centred(key_list[3], (N_SECTION, N_EXP, SEQUENCE_LENGTH, KEY_VALUE_HEADS * HEAD_SIZE), 1.0, 6.0, ((0, 4), (1, 8), (2, 8)))
    out_weight = centred(key_list[4], (N_SECTION, QUERY_HEADS * HEAD_SIZE, D), HEAD_SIZE ** -0.5, 0.5, ((0, 4), (1, 8)))
    norm_gain = jnp.clip(1.0 + 0.1 * jax.random.normal(key_list[5], (N_SECTION, D), jnp.float32), 0.5, 1.5).astype(jnp.bfloat16)
    w_gate = centred(key_list[6], (N_SECTION, EXPERTS, D, FF), D ** -0.5, 0.09375, ((0, 4), (1, 8), (3, 8)))
    w_up = centred(key_list[7], (N_SECTION, EXPERTS, D, FF), D ** -0.5, 0.09375, ((0, 4), (1, 8), (3, 8)))
    w_down_t = centred(key_list[8], (N_SECTION, EXPERTS, D, FF), FF ** -0.5, 0.15625, ((0, 4), (1, 8), (3, 8)))
    expert_ids_keys = jax.random.split(jax.random.fold_in(key_list[9], 1), N_SECTION * N_EXP * SEQUENCE_LENGTH // TOK_DEV)
    expert_ids_turns = jax.random.permutation(jax.random.fold_in(key_list[9], 3), N_SECTION * N_EXP * SEQUENCE_LENGTH // TOK_DEV)
    expert_ids = jax.vmap(lambda own, number: routed_block(jax.random.fold_in(key_list[9], 2), own, number, TOK_DEV, EXPERTS, TOP, CAP, 2))(expert_ids_keys, expert_ids_turns).reshape((N_SECTION, N_EXP, SEQUENCE_LENGTH, TOP))
    route_gates = jnp.clip(jnp.exp(math.log(1.0) - 2.3025851 * jax.random.uniform(key_list[10], (N_SECTION, N_EXP, SEQUENCE_LENGTH, TOP), jnp.float32) ** block_levels(key_list[10], (N_SECTION, N_EXP, SEQUENCE_LENGTH, TOP), ((0, 4), (1, 8), (2, 8)), -0.2, 0.2)), 0.1, 1.0)
    return dict(hidden_in=hidden_in, queries=queries, keys=keys, values=values, out_weight=out_weight, norm_gain=norm_gain, w_gate=w_gate, w_up=w_up, w_down_t=w_down_t, expert_ids=expert_ids, route_gates=route_gates)


def attend_sequence(query_rows, rows_of_key, rows_of_value):
    group_length = QUERY_HEADS // KEY_VALUE_HEADS
    query_heads = query_rows.reshape(SEQUENCE_LENGTH, QUERY_HEADS, HEAD_SIZE).transpose(1, 0, 2)
    heads_of_key = jnp.repeat(rows_of_key.reshape(SEQUENCE_LENGTH, KEY_VALUE_HEADS, HEAD_SIZE).transpose(1, 0, 2), group_length, axis=0)
    heads_of_value = jnp.repeat(rows_of_value.reshape(SEQUENCE_LENGTH, KEY_VALUE_HEADS, HEAD_SIZE).transpose(1, 0, 2), group_length, axis=0)
    position = jnp.arange(SEQUENCE_LENGTH, dtype=jnp.int32)
    causal = position[:, None] >= position[None, :]

    def one_head(operands):
        head_query, head_key, head_value = operands
        scores = jnp.dot(head_query, head_key.T, preferred_element_type=jnp.float32) * (1.0 / math.sqrt(HEAD_SIZE))
        scores = jnp.where(causal, scores, -1e+30)
        shifted = jnp.exp(scores - lax.optimization_barrier(jnp.max(scores, axis=-1, keepdims=True)))
        probs = (shifted / lax.optimization_barrier(jnp.sum(shifted, axis=-1, keepdims=True))).astype(jnp.bfloat16)
        return jnp.dot(probs, head_value, preferred_element_type=jnp.float32).astype(jnp.bfloat16)
    attended = lax.map(one_head, (query_heads, heads_of_key, heads_of_value))
    return attended.transpose(1, 0, 2).reshape(SEQUENCE_LENGTH, QUERY_HEADS * HEAD_SIZE)

def rounded(values_f32):
    return lax.optimization_barrier(values_f32.astype(jnp.bfloat16)).astype(jnp.float32)

def section_layer(rows_in, query_all, key_all, value_all, proj_weight, gain_row, gate_all, up_all, down_all, route_ids, gate_values):
    attended = lax.map(lambda operands: attend_sequence(*operands), (query_all, key_all, value_all))
    flat = attended.reshape(N_EXP * SEQUENCE_LENGTH, QUERY_HEADS * HEAD_SIZE)
    group_cols = QUERY_HEADS * HEAD_SIZE // N_CTX
    attn_proj = jnp.zeros((N_EXP * SEQUENCE_LENGTH, D), jnp.float32)
    for shard in range(N_CTX):
        lower = shard * group_cols
        attn_proj = attn_proj + rounded(jnp.dot(flat[:, lower:lower + group_cols], proj_weight[lower:lower + group_cols], preferred_element_type=jnp.float32))
    residual = rows_in.reshape(N_EXP * SEQUENCE_LENGTH, D).astype(jnp.float32) + attn_proj
    normed = (residual * lax.rsqrt(lax.optimization_barrier(jnp.mean(residual * residual, axis=-1, keepdims=True)) + 1e-06) * gain_row.astype(jnp.float32)).astype(jnp.bfloat16)
    blocks = N_EXP * N_CTX
    per_block = TOK_DEV * TOP
    block_ids = route_ids.reshape(blocks, per_block).astype(jnp.int32)
    onehot = (block_ids[:, :, None] == jnp.arange(N_EXP, dtype=jnp.int32)[None, None, :]).astype(jnp.int32)
    before = (jnp.cumsum(onehot, axis=1).astype(jnp.int32) - onehot) * onehot
    rank = lax.optimization_barrier(jnp.sum(before, axis=-1)).astype(jnp.int32)
    block_index = jnp.broadcast_to(jnp.arange(blocks, dtype=jnp.int32)[:, None], (blocks, per_block))
    route_rows = jnp.repeat(normed, TOP, axis=0).reshape(blocks, per_block, D)
    buffer = jnp.zeros((N_EXP, blocks, CAP, D), jnp.bfloat16).at[block_ids, block_index, rank].set(route_rows)

    def one_expert(operands):
        expert_rows, gate_weight, up_weight, down_weight = operands
        gate_part = jnp.dot(expert_rows, gate_weight, preferred_element_type=jnp.float32)
        up_part = jnp.dot(expert_rows, up_weight, preferred_element_type=jnp.float32)
        hidden = (jax.nn.silu(gate_part) * up_part).astype(jnp.bfloat16)
        shard_units = FF // N_CTX
        summed = jnp.zeros((expert_rows.shape[0], D), jnp.float32)
        for shard in range(N_CTX):
            lower = shard * shard_units
            partial_out = lax.dot_general(hidden[:, lower:lower + shard_units], down_weight[:, lower:lower + shard_units], (((1,), (1,)), ((), ())), preferred_element_type=jnp.float32)
            summed = summed + rounded(partial_out)
        return summed.astype(jnp.bfloat16)
    expert_out = lax.map(one_expert, (buffer.reshape(N_EXP, blocks * CAP, D), gate_all, up_all, down_all))
    expert_out = expert_out.reshape(N_EXP, blocks, CAP, D)
    routed = expert_out[block_ids, block_index, rank].astype(jnp.float32)
    mixture = lax.optimization_barrier(jnp.sum(routed.reshape(N_EXP * SEQUENCE_LENGTH, TOP, D) * gate_values.reshape(N_EXP * SEQUENCE_LENGTH, TOP)[:, :, None], axis=1))
    return (residual + mixture).astype(jnp.bfloat16).reshape(N_EXP, SEQUENCE_LENGTH, D)

def reference(hidden_in, queries, keys, values, out_weight, norm_gain, w_gate, w_up, w_down_t, expert_ids, route_gates):
    outputs = []
    for section_index in range(N_SECTION):
        outputs.append(section_layer(hidden_in[section_index], queries[section_index], keys[section_index], values[section_index], out_weight[section_index], norm_gain[section_index], w_gate[section_index], w_up[section_index], w_down_t[section_index], expert_ids[section_index], route_gates[section_index]))
    return jnp.roll(jnp.stack(outputs), 1, axis=0)
```

```python
import functools
import math

import jax
import jax.numpy as jnp
from jax import lax
from jax.experimental import pallas as pl
from jax.experimental.pallas import tpu as pltpu
from jax.sharding import PartitionSpec as P

MESH = pl.DeviceIdType.MESH

D = 4096
QUERY_HEADS = 32
KEY_VALUE_HEADS = 2
HEAD_SIZE = 128


def passed_along(array, axis, by):
    count = lax.axis_size(axis)
    return lax.ppermute(array, axis, [(i, (i + by) % count) for i in range(count)])

def to_peer(axis, peer, src, dst, send_sem, recv_sem):
    return pltpu.make_async_remote_copy(
        src_ref=src,
        dst_ref=dst,
        send_sem=send_sem,
        recv_sem=recv_sem,
        device_id={axis: peer},
        device_id_type=MESH,
    )


def greet(axis, me, n):
    barrier = pltpu.get_barrier_semaphore()
    for d in range(1, n):
        pl.semaphore_signal(
            barrier, inc=1, device_id={axis: lax.rem(me + d, n)}, device_id_type=MESH
        )
    pl.semaphore_wait(barrier, n - 1)


def moe_kernel(
    n,
    mine,
    gate_any,
    up_any,
    down_any,
    out,
    rows,
    gate,
    up,
    down,
    hid,
    acc,
    obuf,
    load_sem,
    rr_send,
    rr_recv,
    rl_send,
    rl_recv,
    hr_send,
    hr_recv,
    hl_send,
    hl_recv,
    wd_send,
    wd_recv,
    out_send,
    out_recv,
):
    me = lax.axis_index("ctx")
    right, left = lax.rem(me + 1, n), lax.rem(me + n - 1, n)
    half = n // 2
    count, width = mine.shape
    part = out.shape[2]
    units = gate.shape[1]
    pair = count // 2
    loads = [
        pltpu.make_async_copy(gate_any, gate, load_sem.at[0]),
        pltpu.make_async_copy(up_any, up, load_sem.at[1]),
        pltpu.make_async_copy(
            down_any.at[pl.ds(pl.multiple_of(me * part, part), part)], down.at[0], load_sem.at[2]
        ),
    ]
    for load in loads:
        load.start()
    greet("ctx", me, n)

    def slot(r):
        return mine if r == 0 else rows.at[r]

    def rows_step(s):
        cut = width // 2
        if s < half:
            a = to_peer("ctx", right, slot((n + 1 - s) % n), rows.at[n - s], rr_send.at[s - 1], rr_recv.at[s - 1])
            b = to_peer("ctx", left, slot(s - 1), rows.at[s], rl_send.at[s - 1], rl_recv.at[s - 1])
        else:
            a = to_peer(
                "ctx", right, rows.at[n + 1 - s, :, pl.ds(0, cut)], rows.at[n - s, :, pl.ds(0, cut)], rr_send.at[s - 1], rr_recv.at[s - 1]
            )
            b = to_peer(
                "ctx", left, rows.at[s - 1, :, pl.ds(cut, cut)], rows.at[s, :, pl.ds(cut, cut)], rl_send.at[s - 1], rl_recv.at[s - 1]
            )
        return a, b

    def hid_step(s):
        if s < half:
            a = to_peer("ctx", right, hid.at[(n + 1 - s) % n], hid.at[n - s], hr_send.at[s - 1], hr_recv.at[s - 1])
            b = to_peer("ctx", left, hid.at[s - 1], hid.at[s], hl_send.at[s - 1], hl_recv.at[s - 1])
        else:
            a = to_peer(
                "ctx", right, hid.at[n + 1 - s, pl.ds(0, half)], hid.at[n - s, pl.ds(0, half)], hr_send.at[s - 1], hr_recv.at[s - 1]
            )
            b = to_peer(
                "ctx", left, hid.at[s - 1, pl.ds(half, half)], hid.at[s, pl.ds(half, half)], hl_send.at[s - 1], hl_recv.at[s - 1]
            )
        return a, b

    def expand(r):
        block = slot(r)[...]
        gate_part = jnp.dot(block, gate[...], preferred_element_type=jnp.float32)
        up_part = jnp.dot(block, up[...], preferred_element_type=jnp.float32)
        hidden = (gate_part / (1.0 + jnp.exp(-gate_part)) * up_part).astype(jnp.bfloat16)
        owner = lax.rem(me + r, n)
        hid[0, owner, 0:count, :] = hidden[:, 0:128]
        hid[0, owner, count : count + pair, :] = jnp.concatenate(
            [hidden[0:pair, 128:units], hidden[pair:count, 128:units]], axis=1
        )

    def shrink(r, b):
        packed = hid[r, b]
        tail = packed[count : count + pair]
        rest = jnp.concatenate([tail[:, 0 : units - 128], tail[:, units - 128 :]], axis=0)
        hidden = jnp.concatenate([packed[0:count], rest], axis=1)
        return lax.dot_general(
            hidden, down[r], (((1,), (1,)), ((), ())), preferred_element_type=jnp.float32
        )

    sent = list(rows_step(1))
    for copy in sent:
        copy.start()
    downs = []
    for d in (4, 3, 5, 2, 6, 1, 7):
        peer = lax.rem(me + d, n)
        downs.append(
            to_peer(
                "ctx",
                peer,
                down_any.at[pl.ds(pl.multiple_of(peer * part, part), part)],
                down.at[n - d],
                wd_send.at[d - 1],
                wd_recv.at[n - d - 1],
            )
        )
        downs[-1].start()
    loads[0].wait()
    loads[1].wait()
    expand(0)
    now = tuple(sent)
    for s in range(1, half + 1):
        for copy in now:
            copy.wait_recv()
        if s < half:
            now = rows_step(s + 1)
            for copy in now:
                copy.start()
            sent += now
            expand(s)
            expand(n - s)
        else:
            expand(s)
    loads[2].wait()

    now = hid_step(1)
    sent += now
    for copy in now:
        copy.start()
    for copy in downs:
        copy.wait_recv()

    @pl.loop(0, n)
    def _(b):
        acc[b] = shrink(0, b)

    for s in range(1, half):
        for copy in now:
            copy.wait_recv()
        now = hid_step(s + 1)
        sent += now
        for copy in now:
            copy.start()

        @pl.loop(0, n)
        def _(b):
            acc[b] += shrink(s, b) + shrink(n - s, b)

    for copy in now:
        copy.wait_recv()
    for d in (4, 3, 5, 2, 6, 1, 7, 0):
        b = lax.rem(me + d, n)
        block = (acc[b] + shrink(half, b)).astype(jnp.bfloat16)
        if d == 0:
            out[b] = block
        else:
            obuf[d] = block
            copy = to_peer("ctx", b, obuf.at[d], out.at[me], out_send.at[d], out_recv.at[n - d])
            copy.start()
            sent.append(copy)
    for d in range(1, n):
        source = lax.rem(me + d, n)
        to_peer("ctx", source, obuf.at[d], out.at[source], out_send.at[d], out_recv.at[d]).wait_recv()
    for copy in sent + downs:
        copy.wait_send()


def run_experts(mine, gate_shard, up_shard, down_shard):
    n = lax.axis_size("ctx")
    count, width = mine.shape
    units = gate_shard.shape[1]
    part = width // n
    packed = count + count // 2
    dma = pltpu.SemaphoreType.DMA
    anywhere = pl.BlockSpec(memory_space=pl.ANY)
    in_vmem = pl.BlockSpec(memory_space=pltpu.VMEM)
    return pl.pallas_call(
        functools.partial(moe_kernel, n),
        out_shape=jax.ShapeDtypeStruct((n, count, part), jnp.bfloat16),
        in_specs=[in_vmem, anywhere, anywhere, anywhere],
        out_specs=in_vmem,
        scratch_shapes=[
            pltpu.VMEM((n, count, width), jnp.bfloat16),
            pltpu.VMEM((width, units), jnp.bfloat16),
            pltpu.VMEM((width, units), jnp.bfloat16),
            pltpu.VMEM((n, part, units), jnp.bfloat16),
            pltpu.VMEM((n, n, packed, 128), jnp.bfloat16),
            pltpu.VMEM((n, count, part), jnp.float32),
            pltpu.VMEM((n, count, part), jnp.bfloat16),
            dma((3,)),
        ]
        + [dma((n // 2,))] * 8
        + [dma((n - 1,))] * 2
        + [dma((n,))] * 2,
        compiler_params=pltpu.CompilerParams(
            collective_id=0, has_side_effects=True, vmem_limit_bytes=48 * 2**20
        ),
        cost_estimate=pl.CostEstimate(
            flops=6 * n * count * width * units, bytes_accessed=6 * width * units, transcendentals=0
        ),
    )(mine, gate_shard, up_shard, down_shard)


def per_device(
    hidden_in,
    queries,
    keys,
    values,
    out_weight,
    norm_gain,
    w_gate,
    w_up,
    w_down_t,
    expert_ids,
    route_gates,
):
    ctx_count = lax.axis_size("ctx")
    exp_count = lax.axis_size("exp")
    rows_in = hidden_in[0, 0]
    tokens_here = rows_in.shape[0]
    heads_here = QUERY_HEADS // ctx_count
    group_length = QUERY_HEADS // KEY_VALUE_HEADS
    query_split = queries[0, 0].reshape(tokens_here, ctx_count, heads_here * HEAD_SIZE)
    query_local = lax.all_to_all(query_split, "ctx", split_axis=1, concat_axis=0, tiled=True)
    key_all, value_all = (
        lax.all_gather(keys[0, 0], "ctx", axis=0, tiled=True),
        lax.all_gather(values[0, 0], "ctx", axis=0, tiled=True),
    )
    kv_head = lax.axis_index("ctx") * heads_here // group_length
    key_local = lax.dynamic_slice_in_dim(key_all, kv_head * HEAD_SIZE, HEAD_SIZE, 1)
    value_local = lax.dynamic_slice_in_dim(value_all, kv_head * HEAD_SIZE, HEAD_SIZE, 1)
    seq_rows = query_local.shape[0]
    block_rows = min(512, seq_rows)
    block_count = seq_rows // block_rows
    query_blocks = query_local.reshape(block_count, block_rows, heads_here, HEAD_SIZE)
    key_positions = jnp.arange(seq_rows, dtype=jnp.int32)

    def attend_block(operands):
        query_block, first_row = operands
        scores = jnp.einsum(
            "qhd,kd->hqk", query_block, key_local, preferred_element_type=jnp.float32
        ) * (1.0 / math.sqrt(HEAD_SIZE))
        causal = (first_row + jnp.arange(block_rows, dtype=jnp.int32))[:, None] >= key_positions[
            None, :
        ]
        scores = jnp.where(causal[None], scores, -1e30)
        shifted = jnp.exp(scores - jnp.max(scores, axis=-1, keepdims=True))
        probs = (shifted / jnp.sum(shifted, axis=-1, keepdims=True)).astype(jnp.bfloat16)
        mixed = jnp.einsum("hqk,kd->qhd", probs, value_local, preferred_element_type=jnp.float32)
        return mixed.astype(jnp.bfloat16).reshape(block_rows, heads_here * HEAD_SIZE)

    block_starts = jnp.arange(block_count, dtype=jnp.int32) * block_rows
    attended = lax.map(attend_block, (query_blocks, block_starts)).reshape(
        seq_rows, heads_here * HEAD_SIZE
    )
    attn_proj = lax.psum_scatter(
        jnp.dot(attended, out_weight[0], preferred_element_type=jnp.float32).astype(jnp.bfloat16),
        "ctx",
        scatter_dimension=0,
        tiled=True,
    ).astype(jnp.float32)
    residual = rows_in.astype(jnp.float32) + attn_proj
    normed = (
        residual
        * lax.rsqrt(jnp.mean(residual * residual, axis=-1, keepdims=True) + 1e-06)
        * norm_gain[0].astype(jnp.float32)
    ).astype(jnp.bfloat16)
    route_top = expert_ids.shape[-1]
    route_ids = expert_ids[0, 0].reshape(tokens_here * route_top)
    capacity = 5 * tokens_here * route_top // (4 * exp_count)
    onehot = (route_ids[:, None] == jnp.arange(exp_count, dtype=jnp.int32)[None, :]).astype(
        jnp.int32
    )
    rank = jnp.sum((jnp.cumsum(onehot, axis=0) - onehot) * onehot, axis=1)
    slot_of_route = route_ids * capacity + rank
    selector = (
        jnp.arange(exp_count * capacity, dtype=jnp.int32)[:, None] == slot_of_route[None, :]
    ).astype(jnp.bfloat16)
    route_rows = jnp.repeat(normed, route_top, axis=0)
    outgoing = jnp.dot(selector, route_rows, preferred_element_type=jnp.float32).astype(
        jnp.bfloat16
    )
    gate_shard = w_gate[0, 0]
    up_shard = w_up[0, 0]
    down_shard = w_down_t[0, 0]
    arrived = lax.all_to_all(
        outgoing.reshape(exp_count, capacity, D), "exp", split_axis=0, concat_axis=0, tiled=True
    )
    finished = run_experts(
        arrived.reshape(exp_count * capacity, D), gate_shard, up_shard, down_shard
    )
    returned = lax.all_to_all(
        finished.transpose(1, 0, 2).reshape(exp_count, capacity, D),
        "exp",
        split_axis=0,
        concat_axis=0,
        tiled=True,
    )
    expert_out = returned.reshape(exp_count * capacity, D)
    routed = lax.dot_general(
        selector, expert_out, (((0,), (0,)), ((), ())), preferred_element_type=jnp.float32
    )
    mixture = jnp.sum(
        routed.reshape(tokens_here, route_top, D) * route_gates[0, 0][:, :, None], axis=1
    )
    layer_out = (residual + mixture).astype(jnp.bfloat16)
    moved = passed_along(layer_out, "section", 1)
    return moved.reshape(1, 1, tokens_here, D)


def solution(mesh):
    return jax.shard_map(
        per_device,
        mesh=mesh,
        in_specs=(
            P("section", "exp", "ctx", None),
            P("section", "exp", "ctx", None),
            P("section", "exp", "ctx", None),
            P("section", "exp", "ctx", None),
            P("section", "ctx", None),
            P("section", None),
            P("section", "exp", None, "ctx"),
            P("section", "exp", None, "ctx"),
            P("section", "exp", None, "ctx"),
            P("section", "exp", "ctx", None),
            P("section", "exp", "ctx", None),
        ),
        out_specs=P("section", "exp", "ctx", None),
        check_vma=False,
    )
```

```python
import functools
import math

import jax
import jax.numpy as jnp
from jax import lax
from jax.experimental import pallas as pl
from jax.experimental.pallas import tpu as pltpu
from jax.sharding import PartitionSpec as P

D = 4096
QUERY_HEADS = 32
KEY_VALUE_HEADS = 2
HEAD_SIZE = 128
CORES = 2
MESH = pl.DeviceIdType.MESH
BF16, F32, I32 = jnp.bfloat16, jnp.float32, jnp.int32


def to_peer(peer, src, dst, send_sem, recv_sem):
    return pltpu.make_async_remote_copy(
        src_ref=src,
        dst_ref=dst,
        send_sem=send_sem,
        recv_sem=recv_sem,
        device_id=peer,
        device_id_type=MESH,
    )


def greet(peers):
    barrier = pltpu.get_barrier_semaphore()
    for peer in peers:
        pl.semaphore_signal(barrier, inc=1, device_id=peer, device_id_type=MESH)
    pl.semaphore_wait(barrier, len(peers))


def lanes(start, size):
    return pl.ds(pl.multiple_of(start, 128), size)


def across(a, b):
    return lax.dot_general(a, b, (((1,), (1,)), ((), ())), preferred_element_type=F32)


def passed_along(array, axis, by):
    count = lax.axis_size(axis)
    return lax.ppermute(array, axis, [(i, (i + by) % count) for i in range(count)])


def attend_kernel(
    n,
    cols,
    capacity,
    query,
    kv_in,
    ids_in,
    gates_in,
    gain,
    hidden_any,
    weight_any,
    down_any,
    residual,
    mine,
    slots,
    gates,
    down,
    kv,
    mixed,
    weight,
    hidden,
    ids,
    squares,
    bias,
    outgoing,
    local_sem,
    kr_send,
    kr_recv,
    kl_send,
    kl_recv,
    wr_send,
    wr_recv,
    wl_send,
    wl_recv,
    sib_send,
    sib_recv,
    x_send,
    x_recv,
    small_send,
    small_recv,
    sq_send,
    sq_recv,
    out_send,
    out_recv,
    wd_send,
    wd_recv,
):
    z = lax.axis_index("ctx")
    me = lax.axis_index("exp")
    x, core = me // CORES, lax.rem(me, CORES)
    experts = cols * CORES
    half = n // 2
    tokens = query.shape[0]
    width = query.shape[1]
    wide = width // cols
    chunk = width // n
    part = width // n
    heads = chunk // HEAD_SIZE
    group = QUERY_HEADS // KEY_VALUE_HEADS // heads
    up, below = {"ctx": lax.rem(z + 1, n)}, {"ctx": lax.rem(z + n - 1, n)}
    col = [lax.rem(x + d, cols) for d in range(cols)]
    same = [{"exp": col[d] * CORES + core} for d in range(cols)]
    sibling = {"exp": x * CORES + 1 - core}

    locals_ = [
        pltpu.make_async_copy(kv_in, kv.at[z], local_sem.at[0]),
        pltpu.make_async_copy(
            weight_any.at[:, lanes(x * wide, chunk)], weight.at[z, 0], local_sem.at[1]
        ),
        pltpu.make_async_copy(
            weight_any.at[:, lanes(x * wide + chunk, chunk)], weight.at[z, 1], local_sem.at[2]
        ),
        pltpu.make_async_copy(hidden_any.at[:, lanes(x * wide, wide)], hidden.at[x], local_sem.at[3]),
        pltpu.make_async_copy(ids_in, ids.at[x], local_sem.at[4]),
        pltpu.make_async_copy(gates_in, gates.at[x], local_sem.at[5]),
        pltpu.make_async_copy(down_any.at[:, lanes(z * part, part)], down.at[0], local_sem.at[6]),
    ]
    for copy in locals_:
        copy.start()
    greet(
        [{"ctx": lax.rem(z + d, n)} for d in range(1, n)]
        + [{"exp": lax.rem(me + d, experts)} for d in range(1, experts)]
    )

    def kv_step(s):
        a, b = lax.rem(z + n + 1 - s, n), lax.rem(z + s - 1, n)
        cut = tokens // 2
        one, two = kv.at[a], kv.at[b]
        if s == half:
            one, two = kv.at[a, pl.ds(0, cut)], kv.at[b, pl.ds(cut, cut)]
        return (
            to_peer(up, kv_in if s == 1 else one, one, kr_send.at[s - 1], kr_recv.at[s - 1]),
            to_peer(below, kv_in if s == 1 else two, two, kl_send.at[s - 1], kl_recv.at[s - 1]),
        )

    def weight_step(s):
        a, b = lax.rem(z + n + 1 - s, n), lax.rem(z + s - 1, n)
        cut = chunk // 2
        one, two = weight.at[a, core], weight.at[b, core]
        if s == half:
            one, two = weight.at[a, core, pl.ds(0, cut)], weight.at[b, core, pl.ds(cut, cut)]
        own = weight_any.at[:, lanes(x * wide + core * chunk, chunk)]
        return (
            to_peer(up, own if s == 1 else one, one, wr_send.at[s - 1], wr_recv.at[s - 1]),
            to_peer(below, own if s == 1 else two, two, wl_send.at[s - 1], wl_recv.at[s - 1]),
        )

    def share(off):
        k = lax.rem(z + off, n)
        return to_peer(
            sibling, weight.at[k, core], weight.at[k, core], sib_send.at[off], sib_recv.at[off]
        )

    def shared(off):
        k = lax.rem(z + off, n)
        return to_peer(
            sibling, weight.at[k, 1 - core], weight.at[k, 1 - core], sib_send.at[off], sib_recv.at[off]
        )

    def weight_arrived(s):
        for copy in weight_step(s):
            copy.wait_recv()
        if s < half:
            for copy in weight_step(s + 1):
                copy.start()
            share(n - s).start()
        share(s).start()

    small = []
    for d in range(1, cols):
        for at, (src, dst) in enumerate(
            (
                (ids_in, ids.at[x]),
                (gates_in, gates.at[x]),
                (hidden_any.at[:, lanes(col[d] * wide, wide)], hidden.at[x]),
            )
        ):
            small.append(
                to_peer(same[d], src, dst, small_send.at[d, at], small_recv.at[cols - d, at])
            )
    now = kv_step(1)
    for copy in now:
        copy.start()
    for copy in small:
        copy.start()

    row = lax.broadcasted_iota(I32, (tokens, n * tokens), 0) + z * tokens
    column = lax.broadcasted_iota(I32, (tokens, n * tokens), 1)
    bias[...] = jnp.where(row >= column, 0.0, -1e30)
    residual[...] = jnp.zeros_like(residual)

    for s in range(1, half + 1):
        for copy in now:
            copy.wait_recv()
        if s < half:
            now = kv_step(s + 1)
            for copy in now:
                copy.start()
    for copy in weight_step(1):
        copy.start()
    locals_[0].wait()

    def place(j):
        odd = lax.rem(j, 2)
        off = odd * ((j + 1) // 2) + (1 - odd) * lax.rem(n - j // 2, n)
        return off, lax.rem(z + off, n)

    def chunk_first(j):
        _, k = place(j)
        return (
            to_peer(same[1], mixed.at[k, x], mixed.at[k, x], x_send.at[j, 0], x_recv.at[j, 0]),
            to_peer(same[cols - 1], mixed.at[k, x], mixed.at[k, x], x_send.at[j, 1], x_recv.at[j, 1]),
        )

    def chunk_second(j):
        _, k = place(j)
        cut = tokens // 2
        one = mixed.at[k, col[cols - 1], pl.ds(0, cut)]
        two = mixed.at[k, col[1], pl.ds(cut, cut)]
        return (
            to_peer(same[1], one, one, x_send.at[j, 2], x_recv.at[j, 2]),
            to_peer(same[cols - 1], two, two, x_send.at[j, 3], x_recv.at[j, 3]),
        )

    def chunk_forward(j):
        for copy in chunk_first(j):
            copy.wait_recv()
        for copy in chunk_second(j):
            copy.start()

    def project(j):
        off, k = place(j)
        for copy in chunk_second(j):
            copy.wait_recv()

        @pl.when(off > 0)
        def _():
            shared(off).wait_recv()

        rows = mixed[k].reshape(cols * tokens, chunk)
        for side in range(CORES):
            residual[:, side * chunk : (side + 1) * chunk] += jnp.dot(
                rows, weight[k, side], preferred_element_type=F32
            )

    scale = math.log2(math.e) / math.sqrt(HEAD_SIZE)

    @pl.loop(0, n)
    def _(j):
        _, k = place(j)
        kv_head = k // group
        key = kv[:, :, lanes(kv_head * HEAD_SIZE, HEAD_SIZE)].reshape(n * tokens, HEAD_SIZE)
        value = kv[
            :, :, lanes((KEY_VALUE_HEADS + kv_head) * HEAD_SIZE, HEAD_SIZE)
        ].reshape(n * tokens, HEAD_SIZE)
        for h in range(heads):
            scores = across(query[:, lanes(k * chunk + h * HEAD_SIZE, HEAD_SIZE)], key) + bias[...]
            top = jnp.max(scores, axis=-1, keepdims=True)
            shifted = jnp.exp2((scores - top) * scale)
            total = jnp.sum(shifted, axis=-1, keepdims=True)
            out = jnp.dot(shifted.astype(BF16), value, preferred_element_type=F32)
            mixed[k, x, :, h * HEAD_SIZE : (h + 1) * HEAD_SIZE] = (out / total).astype(BF16)
        for copy in chunk_first(j):
            copy.start()

        @pl.when(j >= 1)
        def _():
            chunk_forward(j - 1)

        @pl.when(j == 2)
        def _():
            locals_[1].wait()
            locals_[2].wait()
            weight_arrived(1)

        @pl.when(j == 5)
        def _():
            weight_arrived(2)

        @pl.when(j >= 3)
        def _():
            project(j - 3)

    chunk_forward(n - 1)
    weight_arrived(3)
    project(n - 3)
    project(n - 2)
    weight_arrived(4)
    downs = []
    for d in (4, 3, 5, 2, 6, 1, 7):
        peer = lax.rem(z + d, n)
        downs.append(
            to_peer(
                {"ctx": peer},
                down_any.at[:, lanes(peer * part, part)],
                down.at[n - d],
                wd_send.at[d],
                wd_recv.at[n - d],
            )
        )
        downs[-1].start()
    for copy in small:
        copy.wait_recv()
    for copy in locals_[3:]:
        copy.wait()

    expert = lax.broadcasted_iota(I32, (experts, tokens), 0)
    earlier = lax.broadcasted_iota(I32, (tokens, tokens), 0) < lax.broadcasted_iota(
        I32, (tokens, tokens), 1
    )
    earlier = jnp.where(earlier, 1.0, 0.0).astype(BF16)
    placed = []
    for q in range(cols):
        chosen = ids[q]
        named = jnp.where(expert == chosen, 1.0, 0.0)
        before = jnp.dot(named.astype(BF16), earlier, preferred_element_type=F32)
        rank = jnp.sum(before * named, axis=0, keepdims=True)
        placed.append(
            chosen[0:1] * (cols * capacity) + q * capacity + rank.astype(I32)
        )
    placed = jnp.concatenate(placed, axis=1)
    slots[...] = jnp.broadcast_to(placed, slots.shape)
    slot = lax.broadcasted_iota(I32, (experts * cols * capacity, cols * tokens), 0)
    selector = jnp.where(slot == placed, 1.0, 0.0).astype(BF16)

    project(n - 1)
    residual[...] += hidden[...].reshape(cols * tokens, wide).astype(F32)
    res = residual[...]
    squares[x] = lax.dot_general(
        jnp.ones((8, wide), F32),
        res * res,
        (((1,), (1,)), ((), ())),
        precision=lax.Precision.HIGHEST,
        preferred_element_type=F32,
    )
    sums = [
        to_peer(same[d], squares.at[x], squares.at[x], sq_send.at[d], sq_recv.at[cols - d])
        for d in range(1, cols)
    ]
    for copy in sums:
        copy.start()
    for copy in sums:
        copy.wait_recv()
    total = squares[0]
    for q in range(1, cols):
        total += squares[q]
    inverse = jnp.transpose(lax.rsqrt(total * (1.0 / width) + 1e-06))[:, 0:1]
    normed = (res * inverse * gain[:, lanes(x * wide, wide)].astype(F32)).astype(BF16)
    rows = cols * capacity
    picked = jnp.dot(selector, normed, preferred_element_type=F32).astype(BF16)
    outgoing[...] = picked.reshape(experts, rows, wide)
    sent = []
    for d in (4, 5, 2, 6, 3, 7, 1):
        e = lax.rem(me + d, experts)
        sent.append(
            to_peer(
                {"exp": e},
                outgoing.at[e],
                mine.at[core, :, lanes(x * wide, wide)],
                out_send.at[d],
                out_recv.at[experts - d],
            )
        )
        sent[-1].start()
    keep = pltpu.make_async_copy(
        outgoing.at[me], mine.at[core, :, lanes(x * wide, wide)], local_sem.at[0]
    )
    keep.start()
    keep.wait()
    for copy in sent:
        copy.wait_recv()
    for copy in downs:
        copy.wait_recv()

    for copy in small + sums + sent + downs:
        copy.wait_send()
    for s in range(1, half + 1):
        for copy in kv_step(s) + weight_step(s):
            copy.wait_send()
    for off in range(1, n):
        share(off).wait_send()

    @pl.loop(0, n)
    def _(j):
        for copy in chunk_first(j) + chunk_second(j):
            copy.wait_send()


def run_attend(query, kv, ids, gates, gain, hidden, weight, down, capacity):
    n = lax.axis_size("ctx")
    experts = lax.axis_size("exp")
    cols = experts // CORES
    tokens, width = query.shape
    wide, part = width // cols, width // n
    units = down.shape[0]
    dma = pltpu.SemaphoreType.DMA
    anywhere = pl.BlockSpec(memory_space=pl.ANY)
    in_vmem = pl.BlockSpec(memory_space=pltpu.VMEM)
    shape = jax.ShapeDtypeStruct
    return pl.pallas_call(
        functools.partial(attend_kernel, n, cols, capacity),
        out_shape=(
            shape((cols * tokens, wide), F32),
            shape((CORES, cols * capacity, width), BF16),
            shape((8, cols * tokens), I32),
            shape((cols, tokens, 128), F32),
            shape((n, units, part), BF16),
        ),
        in_specs=[in_vmem] * 5 + [anywhere] * 3,
        out_specs=(in_vmem,) * 5,
        scratch_shapes=[
            pltpu.VMEM((n, tokens, kv.shape[1]), BF16),
            pltpu.VMEM((n, cols, tokens, width // n), BF16),
            pltpu.VMEM((n, CORES, width // n, width // n), BF16),
            pltpu.VMEM((cols, tokens, wide), BF16),
            pltpu.VMEM((cols, 8, tokens), I32),
            pltpu.VMEM((cols, 8, cols * tokens), F32),
            pltpu.VMEM((tokens, n * tokens), F32),
            pltpu.VMEM((experts, cols * capacity, wide), BF16),
            dma((7,)),
        ]
        + [dma((n // 2,))] * 8
        + [dma((n,))] * 2
        + [dma((n, 4))] * 2
        + [dma((cols, 3))] * 2
        + [dma((cols,))] * 2
        + [dma((experts,))] * 2
        + [dma((n,))] * 2,
        compiler_params=pltpu.CompilerParams(
            collective_id=1, has_side_effects=True, vmem_limit_bytes=56 * 2**20
        ),
        cost_estimate=pl.CostEstimate(
            flops=2 * cols * tokens * width * wide,
            bytes_accessed=8 * 2**20,
            transcendentals=QUERY_HEADS * tokens * n * tokens,
        ),
    )(query, kv, ids, gates, gain, hidden, weight, down)


def moe_kernel(
    n,
    mine,
    down,
    gate_any,
    up_any,
    out,
    rows,
    gate,
    up,
    hid,
    acc,
    obuf,
    load_sem,
    rr_send,
    rr_recv,
    rl_send,
    rl_recv,
    hr_send,
    hr_recv,
    hl_send,
    hl_recv,
    out_send,
    out_recv,
):
    me = lax.axis_index("ctx")
    right, left = {"ctx": lax.rem(me + 1, n)}, {"ctx": lax.rem(me + n - 1, n)}
    half = n // 2
    count, width = mine.shape
    units = gate.shape[0]
    pair = count // 2
    loads = [
        pltpu.make_async_copy(gate_any, gate, load_sem.at[0]),
        pltpu.make_async_copy(up_any, up, load_sem.at[1]),
    ]
    for load in loads:
        load.start()
    greet([{"ctx": lax.rem(me + d, n)} for d in range(1, n)])

    def slot(r):
        return mine if r == 0 else rows.at[r]

    def rows_step(s):
        cut = width // 2
        if s < half:
            a = to_peer(right, slot((n + 1 - s) % n), rows.at[n - s], rr_send.at[s - 1], rr_recv.at[s - 1])
            b = to_peer(left, slot(s - 1), rows.at[s], rl_send.at[s - 1], rl_recv.at[s - 1])
        else:
            a = to_peer(
                right, rows.at[n + 1 - s, :, pl.ds(0, cut)], rows.at[n - s, :, pl.ds(0, cut)], rr_send.at[s - 1], rr_recv.at[s - 1]
            )
            b = to_peer(
                left, rows.at[s - 1, :, pl.ds(cut, cut)], rows.at[s, :, pl.ds(cut, cut)], rl_send.at[s - 1], rl_recv.at[s - 1]
            )
        return a, b

    def hid_step(s):
        if s < half:
            a = to_peer(right, hid.at[(n + 1 - s) % n], hid.at[n - s], hr_send.at[s - 1], hr_recv.at[s - 1])
            b = to_peer(left, hid.at[s - 1], hid.at[s], hl_send.at[s - 1], hl_recv.at[s - 1])
        else:
            a = to_peer(
                right, hid.at[n + 1 - s, pl.ds(0, half)], hid.at[n - s, pl.ds(0, half)], hr_send.at[s - 1], hr_recv.at[s - 1]
            )
            b = to_peer(
                left, hid.at[s - 1, pl.ds(half, half)], hid.at[s, pl.ds(half, half)], hl_send.at[s - 1], hl_recv.at[s - 1]
            )
        return a, b

    def expand(r):
        block = slot(r)[...]
        gate_part = across(block, gate[...])
        up_part = across(block, up[...])
        hidden = (gate_part / (1.0 + jnp.exp(-gate_part)) * up_part).astype(BF16)
        owner = lax.rem(me + r, n)
        hid[0, owner, 0:count, :] = hidden[:, 0:128]
        hid[0, owner, count : count + pair, :] = jnp.concatenate(
            [hidden[0:pair, 128:units], hidden[pair:count, 128:units]], axis=1
        )

    def shrink(r, b):
        packed = hid[r, b]
        tail = packed[count : count + pair]
        rest = jnp.concatenate([tail[:, 0 : units - 128], tail[:, units - 128 :]], axis=0)
        hidden = jnp.concatenate([packed[0:count], rest], axis=1)
        return jnp.dot(hidden, down[r], preferred_element_type=F32)

    now = rows_step(1)
    sent = list(now)
    for copy in now:
        copy.start()
    for load in loads:
        load.wait()
    expand(0)
    for s in range(1, half + 1):
        for copy in now:
            copy.wait_recv()
        if s < half:
            now = rows_step(s + 1)
            for copy in now:
                copy.start()
            sent += now
            expand(s)
            expand(n - s)
        else:
            expand(s)

    now = hid_step(1)
    sent += now
    for copy in now:
        copy.start()

    @pl.loop(0, n)
    def _(b):
        acc[b] = shrink(0, b)

    for s in range(1, half):
        for copy in now:
            copy.wait_recv()
        now = hid_step(s + 1)
        sent += now
        for copy in now:
            copy.start()

        @pl.loop(0, n)
        def _(b):
            acc[b] += shrink(s, b) + shrink(n - s, b)

    for copy in now:
        copy.wait_recv()
    for d in (4, 3, 5, 2, 6, 1, 7, 0):
        b = lax.rem(me + d, n)
        block = (acc[b] + shrink(half, b)).astype(BF16)
        if d == 0:
            out[b] = block
        else:
            obuf[d] = block
            copy = to_peer({"ctx": b}, obuf.at[d], out.at[me], out_send.at[d], out_recv.at[n - d])
            copy.start()
            sent.append(copy)
    for d in range(1, n):
        source = lax.rem(me + d, n)
        to_peer(
            {"ctx": source}, obuf.at[d], out.at[source], out_send.at[d], out_recv.at[d]
        ).wait_recv()
    for copy in sent:
        copy.wait_send()


def run_experts(mine, down, gate_shard, up_shard):
    n = lax.axis_size("ctx")
    count, width = mine.shape
    units = gate_shard.shape[0]
    part = width // n
    packed = count + count // 2
    dma = pltpu.SemaphoreType.DMA
    anywhere = pl.BlockSpec(memory_space=pl.ANY)
    in_vmem = pl.BlockSpec(memory_space=pltpu.VMEM)
    return pl.pallas_call(
        functools.partial(moe_kernel, n),
        out_shape=jax.ShapeDtypeStruct((n, count, part), BF16),
        in_specs=[in_vmem, in_vmem, anywhere, anywhere],
        out_specs=in_vmem,
        scratch_shapes=[
            pltpu.VMEM((n, count, width), BF16),
            pltpu.VMEM((units, width), BF16),
            pltpu.VMEM((units, width), BF16),
            pltpu.VMEM((n, n, packed, 128), BF16),
            pltpu.VMEM((n, count, part), F32),
            pltpu.VMEM((n, count, part), BF16),
            dma((2,)),
        ]
        + [dma((n // 2,))] * 8
        + [dma((n,))] * 2,
        compiler_params=pltpu.CompilerParams(
            collective_id=0, has_side_effects=True, vmem_limit_bytes=48 * 2**20
        ),
        cost_estimate=pl.CostEstimate(
            flops=6 * n * count * width * units, bytes_accessed=6 * width * units, transcendentals=0
        ),
    )(mine, down, gate_shard, up_shard)


def per_device(
    hidden_in,
    queries,
    keys,
    values,
    out_weight,
    norm_gain,
    w_gate,
    w_up,
    w_down_t,
    expert_ids,
    route_gates,
):
    ctx_count = lax.axis_size("ctx")
    exp_count = lax.axis_size("exp")
    cols = exp_count // CORES
    tokens_here = hidden_in.shape[2]
    capacity = 5 * tokens_here // (4 * exp_count)
    wide = D // cols
    part = D // ctx_count
    ids = jnp.broadcast_to(expert_ids[0, 0].reshape(1, tokens_here), (exp_count, tokens_here))
    gates = jnp.broadcast_to(route_gates[0, 0], (tokens_here, 128))
    residual, mine, slots, gates_all, down = run_attend(
        queries[0, 0],
        jnp.concatenate([keys[0, 0], values[0, 0]], axis=1),
        ids,
        gates,
        norm_gain,
        hidden_in[0, 0],
        out_weight[0],
        w_down_t[0, 0].T,
        capacity,
    )
    finished = run_experts(
        mine.reshape(exp_count * capacity, D), down, w_gate[0, 0].T, w_up[0, 0].T
    )
    rows = cols * capacity
    leaving = (
        finished.reshape(cols, ctx_count // cols, CORES, rows, part)
        .transpose(0, 2, 3, 1, 4)
        .reshape(exp_count, rows, wide)
    )
    returned = lax.all_to_all(leaving, "exp", split_axis=0, concat_axis=0, tiled=True)
    selector = (
        jnp.arange(exp_count * rows, dtype=I32)[:, None] == slots[0:1]
    ).astype(BF16)
    routed = lax.dot_general(
        selector,
        returned.reshape(exp_count * rows, wide),
        (((0,), (0,)), ((), ())),
        preferred_element_type=F32,
    )
    mixture = routed * gates_all[:, :, 0].reshape(cols * tokens_here, 1)
    layer_out = (residual + mixture).astype(BF16).reshape(cols, tokens_here, wide)
    groups = [[q * CORES + c for q in range(cols)] for c in range(CORES)]
    owned = lax.all_to_all(
        layer_out, "exp", split_axis=0, concat_axis=0, tiled=True, axis_index_groups=groups
    )
    owned = owned.transpose(1, 0, 2).reshape(tokens_here, D)
    moved = passed_along(owned, "section", 1)
    return moved.reshape(1, 1, tokens_here, D)


def solution(mesh):
    return jax.shard_map(
        per_device,
        mesh=mesh,
        in_specs=(
            P("section", "exp", "ctx", None),
            P("section", "exp", "ctx", None),
            P("section", "exp", "ctx", None),
            P("section", "exp", "ctx", None),
            P("section", "ctx", None),
            P("section", None),
            P("section", "exp", None, "ctx"),
            P("section", "exp", None, "ctx"),
            P("section", "exp", None, "ctx"),
            P("section", "exp", "ctx", None),
            P("section", "exp", "ctx", None),
        ),
        out_specs=P("section", "exp", "ctx", None),
        check_vma=False,
    )
```

```python
import functools
import math

import jax
import jax.numpy as jnp
from jax import lax
from jax.experimental import pallas as pl
from jax.experimental.pallas import tpu as pltpu
from jax.sharding import PartitionSpec as P

D = 4096
QUERY_HEADS = 32
KEY_VALUE_HEADS = 2
HEAD_SIZE = 128
CORES = 2
MESH = pl.DeviceIdType.MESH
BF16, F32, I32 = jnp.bfloat16, jnp.float32, jnp.int32


def to_peer(peer, src, dst, send_sem, recv_sem):
    return pltpu.make_async_remote_copy(
        src_ref=src,
        dst_ref=dst,
        send_sem=send_sem,
        recv_sem=recv_sem,
        device_id=peer,
        device_id_type=MESH,
    )


def greet(peers):
    barrier = pltpu.get_barrier_semaphore()
    for peer in peers:
        pl.semaphore_signal(barrier, inc=1, device_id=peer, device_id_type=MESH)
    pl.semaphore_wait(barrier, len(peers))


def lanes(start, size):
    return pl.ds(pl.multiple_of(start, 128), size)


def across(a, b):
    return lax.dot_general(a, b, (((1,), (1,)), ((), ())), preferred_element_type=F32)


def attend_kernel(
    n,
    cols,
    capacity,
    query,
    kv_in,
    ids_in,
    gates_in,
    gain,
    hidden_any,
    weight_any,
    down_any,
    residual,
    mine,
    slots,
    gates,
    down,
    kv,
    mixed,
    weight,
    hidden,
    ids,
    squares,
    bias,
    outgoing,
    local_sem,
    kr_send,
    kr_recv,
    kl_send,
    kl_recv,
    wr_send,
    wr_recv,
    wl_send,
    wl_recv,
    sib_send,
    sib_recv,
    x_send,
    x_recv,
    small_send,
    small_recv,
    sq_send,
    sq_recv,
    out_send,
    out_recv,
    wd_send,
    wd_recv,
):
    z = lax.axis_index("ctx")
    me = lax.axis_index("exp")
    x, core = me // CORES, lax.rem(me, CORES)
    experts = cols * CORES
    half = n // 2
    tokens = query.shape[0]
    width = query.shape[1]
    wide = width // cols
    chunk = width // n
    part = width // n
    heads = chunk // HEAD_SIZE
    group = QUERY_HEADS // KEY_VALUE_HEADS // heads
    up, below = {"ctx": lax.rem(z + 1, n)}, {"ctx": lax.rem(z + n - 1, n)}
    col = [lax.rem(x + d, cols) for d in range(cols)]
    same = [{"exp": col[d] * CORES + core} for d in range(cols)]
    sibling = {"exp": x * CORES + 1 - core}

    locals_ = [
        pltpu.make_async_copy(kv_in, kv.at[z], local_sem.at[0]),
        pltpu.make_async_copy(
            weight_any.at[:, lanes(x * wide, chunk)], weight.at[z, 0], local_sem.at[1]
        ),
        pltpu.make_async_copy(
            weight_any.at[:, lanes(x * wide + chunk, chunk)], weight.at[z, 1], local_sem.at[2]
        ),
        pltpu.make_async_copy(hidden_any.at[:, lanes(x * wide, wide)], hidden.at[x], local_sem.at[3]),
        pltpu.make_async_copy(ids_in, ids.at[x], local_sem.at[4]),
        pltpu.make_async_copy(gates_in, gates.at[x], local_sem.at[5]),
        pltpu.make_async_copy(down_any.at[:, lanes(z * part, part)], down.at[0], local_sem.at[6]),
    ]
    for copy in locals_:
        copy.start()
    greet(
        [{"ctx": lax.rem(z + d, n)} for d in range(1, n)]
        + [{"exp": lax.rem(me + d, experts)} for d in range(1, experts)]
    )

    def kv_step(s):
        a, b = lax.rem(z + n + 1 - s, n), lax.rem(z + s - 1, n)
        cut = tokens // 2
        one, two = kv.at[a], kv.at[b]
        if s == half:
            one, two = kv.at[a, pl.ds(0, cut)], kv.at[b, pl.ds(cut, cut)]
        return (
            to_peer(up, kv_in if s == 1 else one, one, kr_send.at[s - 1], kr_recv.at[s - 1]),
            to_peer(below, kv_in if s == 1 else two, two, kl_send.at[s - 1], kl_recv.at[s - 1]),
        )

    def weight_step(s):
        a, b = lax.rem(z + n + 1 - s, n), lax.rem(z + s - 1, n)
        cut = chunk // 2
        one, two = weight.at[a, core], weight.at[b, core]
        if s == half:
            one, two = weight.at[a, core, pl.ds(0, cut)], weight.at[b, core, pl.ds(cut, cut)]
        own = weight_any.at[:, lanes(x * wide + core * chunk, chunk)]
        return (
            to_peer(up, own if s == 1 else one, one, wr_send.at[s - 1], wr_recv.at[s - 1]),
            to_peer(below, own if s == 1 else two, two, wl_send.at[s - 1], wl_recv.at[s - 1]),
        )

    def share(off):
        k = lax.rem(z + off, n)
        return to_peer(
            sibling, weight.at[k, core], weight.at[k, core], sib_send.at[off], sib_recv.at[off]
        )

    def shared(off):
        k = lax.rem(z + off, n)
        return to_peer(
            sibling, weight.at[k, 1 - core], weight.at[k, 1 - core], sib_send.at[off], sib_recv.at[off]
        )

    def weight_arrived(s):
        for copy in weight_step(s):
            copy.wait_recv()
        if s < half:
            for copy in weight_step(s + 1):
                copy.start()
            share(n - s).start()
        share(s).start()

    small = []
    for d in range(1, cols):
        for at, (src, dst) in enumerate(
            (
                (ids_in, ids.at[x]),
                (gates_in, gates.at[x]),
                (hidden_any.at[:, lanes(col[d] * wide, wide)], hidden.at[x]),
            )
        ):
            small.append(
                to_peer(same[d], src, dst, small_send.at[d, at], small_recv.at[cols - d, at])
            )
    now = kv_step(1)
    for copy in now:
        copy.start()
    for copy in small:
        copy.start()

    row = lax.broadcasted_iota(I32, (tokens, n * tokens), 0) + z * tokens
    column = lax.broadcasted_iota(I32, (tokens, n * tokens), 1)
    bias[...] = jnp.where(row >= column, 0.0, -1e30)
    residual[...] = jnp.zeros_like(residual)

    for s in range(1, half + 1):
        for copy in now:
            copy.wait_recv()
        if s < half:
            now = kv_step(s + 1)
            for copy in now:
                copy.start()
    for copy in weight_step(1):
        copy.start()
    locals_[0].wait()

    def place(j):
        odd = lax.rem(j, 2)
        off = odd * ((j + 1) // 2) + (1 - odd) * lax.rem(n - j // 2, n)
        return off, lax.rem(z + off, n)

    def chunk_first(j):
        _, k = place(j)
        return (
            to_peer(same[1], mixed.at[k, x], mixed.at[k, x], x_send.at[j, 0], x_recv.at[j, 0]),
            to_peer(same[cols - 1], mixed.at[k, x], mixed.at[k, x], x_send.at[j, 1], x_recv.at[j, 1]),
        )

    def chunk_second(j):
        _, k = place(j)
        cut = tokens // 2
        one = mixed.at[k, col[cols - 1], pl.ds(0, cut)]
        two = mixed.at[k, col[1], pl.ds(cut, cut)]
        return (
            to_peer(same[1], one, one, x_send.at[j, 2], x_recv.at[j, 2]),
            to_peer(same[cols - 1], two, two, x_send.at[j, 3], x_recv.at[j, 3]),
        )

    def chunk_forward(j):
        for copy in chunk_first(j):
            copy.wait_recv()
        for copy in chunk_second(j):
            copy.start()

    def project(j):
        off, k = place(j)
        for copy in chunk_second(j):
            copy.wait_recv()

        @pl.when(off > 0)
        def _():
            shared(off).wait_recv()

        rows = mixed[k].reshape(cols * tokens, chunk)
        for side in range(CORES):
            residual[:, side * chunk : (side + 1) * chunk] += jnp.dot(
                rows, weight[k, side], preferred_element_type=F32
            )

    scale = math.log2(math.e) / math.sqrt(HEAD_SIZE)

    @pl.loop(0, n)
    def _(j):
        _, k = place(j)
        kv_head = k // group
        key = kv[:, :, lanes(kv_head * HEAD_SIZE, HEAD_SIZE)].reshape(n * tokens, HEAD_SIZE)
        value = kv[
            :, :, lanes((KEY_VALUE_HEADS + kv_head) * HEAD_SIZE, HEAD_SIZE)
        ].reshape(n * tokens, HEAD_SIZE)
        for h in range(heads):
            scores = across(query[:, lanes(k * chunk + h * HEAD_SIZE, HEAD_SIZE)], key) + bias[...]
            top = jnp.max(scores, axis=-1, keepdims=True)
            shifted = jnp.exp2((scores - top) * scale)
            total = jnp.sum(shifted, axis=-1, keepdims=True)
            out = jnp.dot(shifted.astype(BF16), value, preferred_element_type=F32)
            mixed[k, x, :, h * HEAD_SIZE : (h + 1) * HEAD_SIZE] = (out / total).astype(BF16)
        for copy in chunk_first(j):
            copy.start()

        @pl.when(j >= 1)
        def _():
            chunk_forward(j - 1)

        @pl.when(j == 2)
        def _():
            locals_[1].wait()
            locals_[2].wait()
            weight_arrived(1)

        @pl.when(j == 5)
        def _():
            weight_arrived(2)

        @pl.when(j >= 3)
        def _():
            project(j - 3)

    chunk_forward(n - 1)
    weight_arrived(3)
    project(n - 3)
    project(n - 2)
    weight_arrived(4)
    downs = []
    for d in (4, 3, 5, 2, 6, 1, 7):
        peer = lax.rem(z + d, n)
        downs.append(
            to_peer(
                {"ctx": peer},
                down_any.at[:, lanes(peer * part, part)],
                down.at[n - d],
                wd_send.at[d],
                wd_recv.at[n - d],
            )
        )
        downs[-1].start()
    for copy in small:
        copy.wait_recv()
    for copy in locals_[3:]:
        copy.wait()

    expert = lax.broadcasted_iota(I32, (experts, tokens), 0)
    earlier = lax.broadcasted_iota(I32, (tokens, tokens), 0) < lax.broadcasted_iota(
        I32, (tokens, tokens), 1
    )
    earlier = jnp.where(earlier, 1.0, 0.0).astype(BF16)
    placed = []
    for q in range(cols):
        chosen = ids[q]
        named = jnp.where(expert == chosen, 1.0, 0.0)
        before = jnp.dot(named.astype(BF16), earlier, preferred_element_type=F32)
        rank = jnp.sum(before * named, axis=0, keepdims=True)
        placed.append(
            chosen[0:1] * (cols * capacity) + q * capacity + rank.astype(I32)
        )
    placed = jnp.concatenate(placed, axis=1)
    slots[...] = jnp.broadcast_to(placed, slots.shape)
    slot = lax.broadcasted_iota(I32, (experts * cols * capacity, cols * tokens), 0)
    selector = jnp.where(slot == placed, 1.0, 0.0).astype(BF16)

    project(n - 1)
    residual[...] += hidden[...].reshape(cols * tokens, wide).astype(F32)
    res = residual[...]
    squares[x] = lax.dot_general(
        jnp.ones((8, wide), F32),
        res * res,
        (((1,), (1,)), ((), ())),
        precision=lax.Precision.HIGHEST,
        preferred_element_type=F32,
    )
    sums = [
        to_peer(same[d], squares.at[x], squares.at[x], sq_send.at[d], sq_recv.at[cols - d])
        for d in range(1, cols)
    ]
    for copy in sums:
        copy.start()
    for copy in sums:
        copy.wait_recv()
    total = squares[0]
    for q in range(1, cols):
        total += squares[q]
    inverse = jnp.transpose(lax.rsqrt(total * (1.0 / width) + 1e-06))[:, 0:1]
    normed = (res * inverse * gain[:, lanes(x * wide, wide)].astype(F32)).astype(BF16)
    rows = cols * capacity
    picked = jnp.dot(selector, normed, preferred_element_type=F32).astype(BF16)
    outgoing[...] = picked.reshape(experts, rows, wide)
    sent = []
    for d in (4, 5, 2, 6, 3, 7, 1):
        e = lax.rem(me + d, experts)
        sent.append(
            to_peer(
                {"exp": e},
                outgoing.at[e],
                mine.at[core, :, lanes(x * wide, wide)],
                out_send.at[d],
                out_recv.at[experts - d],
            )
        )
        sent[-1].start()
    keep = pltpu.make_async_copy(
        outgoing.at[me], mine.at[core, :, lanes(x * wide, wide)], local_sem.at[0]
    )
    keep.start()
    keep.wait()
    for copy in sent:
        copy.wait_recv()
    for copy in downs:
        copy.wait_recv()

    for copy in small + sums + sent + downs:
        copy.wait_send()
    for s in range(1, half + 1):
        for copy in kv_step(s) + weight_step(s):
            copy.wait_send()
    for off in range(1, n):
        share(off).wait_send()

    @pl.loop(0, n)
    def _(j):
        for copy in chunk_first(j) + chunk_second(j):
            copy.wait_send()


def run_attend(query, kv, ids, gates, gain, hidden, weight, down, capacity):
    n = lax.axis_size("ctx")
    experts = lax.axis_size("exp")
    cols = experts // CORES
    tokens, width = query.shape
    wide, part = width // cols, width // n
    units = down.shape[0]
    dma = pltpu.SemaphoreType.DMA
    anywhere = pl.BlockSpec(memory_space=pl.ANY)
    in_vmem = pl.BlockSpec(memory_space=pltpu.VMEM)
    shape = jax.ShapeDtypeStruct
    return pl.pallas_call(
        functools.partial(attend_kernel, n, cols, capacity),
        out_shape=(
            shape((cols * tokens, wide), F32),
            shape((CORES, cols * capacity, width), BF16),
            shape((8, cols * tokens), I32),
            shape((cols, tokens, 128), F32),
            shape((n, units, part), BF16),
        ),
        in_specs=[in_vmem] * 5 + [anywhere] * 3,
        out_specs=(in_vmem,) * 5,
        scratch_shapes=[
            pltpu.VMEM((n, tokens, kv.shape[1]), BF16),
            pltpu.VMEM((n, cols, tokens, width // n), BF16),
            pltpu.VMEM((n, CORES, width // n, width // n), BF16),
            pltpu.VMEM((cols, tokens, wide), BF16),
            pltpu.VMEM((cols, 8, tokens), I32),
            pltpu.VMEM((cols, 8, cols * tokens), F32),
            pltpu.VMEM((tokens, n * tokens), F32),
            pltpu.VMEM((experts, cols * capacity, wide), BF16),
            dma((7,)),
        ]
        + [dma((n // 2,))] * 8
        + [dma((n,))] * 2
        + [dma((n, 4))] * 2
        + [dma((cols, 3))] * 2
        + [dma((cols,))] * 2
        + [dma((experts,))] * 2
        + [dma((n,))] * 2,
        compiler_params=pltpu.CompilerParams(
            collective_id=1, has_side_effects=True, vmem_limit_bytes=56 * 2**20
        ),
        cost_estimate=pl.CostEstimate(
            flops=2 * cols * tokens * width * wide,
            bytes_accessed=8 * 2**20,
            transcendentals=QUERY_HEADS * tokens * n * tokens,
        ),
    )(query, kv, ids, gates, gain, hidden, weight, down)


def moe_kernel(
    n,
    sections,
    mine,
    down,
    residual,
    slots,
    gates,
    gate_any,
    up_any,
    result,
    out,
    back,
    stage,
    selector,
    rows,
    gate,
    up,
    hid,
    acc,
    obuf,
    load_sem,
    rr_send,
    rr_recv,
    rl_send,
    rl_recv,
    hr_send,
    hr_recv,
    hl_send,
    hl_recv,
    out_send,
    out_recv,
    back_send,
    back_recv,
    last_send,
    last_recv,
):
    me = lax.axis_index("ctx")
    mine_exp = lax.axis_index("exp")
    section = lax.axis_index("section")
    x, core = mine_exp // CORES, lax.rem(mine_exp, CORES)
    cols, tokens = gates.shape[0], gates.shape[1]
    experts = cols * CORES
    per_col = n // cols
    part = out.shape[2]
    block_rows = back.shape[1]
    after, before = lax.rem(section + 1, sections), lax.rem(section + sections - 1, sections)
    right, left = {"ctx": lax.rem(me + 1, n)}, {"ctx": lax.rem(me + n - 1, n)}
    half = n // 2
    count, width = mine.shape
    units = gate.shape[0]
    pair = count // 2
    loads = [
        pltpu.make_async_copy(gate_any, gate, load_sem.at[0]),
        pltpu.make_async_copy(up_any, up, load_sem.at[1]),
    ]
    for load in loads:
        load.start()
    greet(
        [{"ctx": lax.rem(me + d, n)} for d in range(1, n)]
        + [{"exp": lax.rem(mine_exp + d, experts)} for d in range(1, experts)]
        + [{"section": at, "exp": q * CORES + core} for at in (after, before) for q in range(cols)]
    )

    def slot(r):
        return mine if r == 0 else rows.at[r]

    def rows_step(s):
        cut = width // 2
        if s < half:
            a = to_peer(right, slot((n + 1 - s) % n), rows.at[n - s], rr_send.at[s - 1], rr_recv.at[s - 1])
            b = to_peer(left, slot(s - 1), rows.at[s], rl_send.at[s - 1], rl_recv.at[s - 1])
        else:
            a = to_peer(
                right, rows.at[n + 1 - s, :, pl.ds(0, cut)], rows.at[n - s, :, pl.ds(0, cut)], rr_send.at[s - 1], rr_recv.at[s - 1]
            )
            b = to_peer(
                left, rows.at[s - 1, :, pl.ds(cut, cut)], rows.at[s, :, pl.ds(cut, cut)], rl_send.at[s - 1], rl_recv.at[s - 1]
            )
        return a, b

    def hid_step(s):
        if s < half:
            a = to_peer(right, hid.at[(n + 1 - s) % n], hid.at[n - s], hr_send.at[s - 1], hr_recv.at[s - 1])
            b = to_peer(left, hid.at[s - 1], hid.at[s], hl_send.at[s - 1], hl_recv.at[s - 1])
        else:
            a = to_peer(
                right, hid.at[n + 1 - s, pl.ds(0, half)], hid.at[n - s, pl.ds(0, half)], hr_send.at[s - 1], hr_recv.at[s - 1]
            )
            b = to_peer(
                left, hid.at[s - 1, pl.ds(half, half)], hid.at[s, pl.ds(half, half)], hl_send.at[s - 1], hl_recv.at[s - 1]
            )
        return a, b

    def expand(r):
        block = slot(r)[...]
        gate_part = across(block, gate[...])
        up_part = across(block, up[...])
        hidden = (gate_part / (1.0 + jnp.exp(-gate_part)) * up_part).astype(BF16)
        owner = lax.rem(me + r, n)
        hid[0, owner, 0:count, :] = hidden[:, 0:128]
        hid[0, owner, count : count + pair, :] = jnp.concatenate(
            [hidden[0:pair, 128:units], hidden[pair:count, 128:units]], axis=1
        )

    def shrink(r, b):
        packed = hid[r, b]
        tail = packed[count : count + pair]
        rest = jnp.concatenate([tail[:, 0 : units - 128], tail[:, units - 128 :]], axis=0)
        hidden = jnp.concatenate([packed[0:count], rest], axis=1)
        return jnp.dot(hidden, down[r], preferred_element_type=F32)

    now = rows_step(1)
    sent = list(now)
    for copy in now:
        copy.start()
    for load in loads:
        load.wait()
    expand(0)
    slot_row = lax.broadcasted_iota(I32, selector.shape, 0)
    selector[...] = jnp.where(slot_row == slots[0:1], 1.0, 0.0).astype(BF16)
    for s in range(1, half + 1):
        for copy in now:
            copy.wait_recv()
        if s < half:
            now = rows_step(s + 1)
            for copy in now:
                copy.start()
            sent += now
            expand(s)
            expand(n - s)
        else:
            expand(s)

    now = hid_step(1)
    sent += now
    for copy in now:
        copy.start()

    @pl.loop(0, n)
    def _(b):
        acc[b] = shrink(0, b)

    for s in range(1, half):
        for copy in now:
            copy.wait_recv()
        now = hid_step(s + 1)
        sent += now
        for copy in now:
            copy.start()

        @pl.loop(0, n)
        def _(b):
            acc[b] += shrink(s, b) + shrink(n - s, b)

    for copy in now:
        copy.wait_recv()

    def finish(d):
        b = lax.rem(me + d, n)
        block = (acc[b] + shrink(half, b)).astype(BF16)
        if d == 0:
            out[me] = block
        else:
            obuf[d] = block
            copy = to_peer({"ctx": b}, obuf.at[d], out.at[me], out_send.at[d], out_recv.at[n - d])
            copy.start()
            sent.append(copy)

    def hand_back(r, c):
        source = lax.rem(me + r, n)
        owner = source // per_col * CORES + c
        side = lax.rem(source, per_col)
        rel = lax.rem(mine_exp - owner + experts, experts)
        src = out.at[source, pl.ds(c * block_rows, block_rows)]
        dst = back.at[mine_exp, :, lanes(side * part, part)]
        there = to_peer({"exp": owner}, src, dst, back_send.at[r, c], back_recv.at[rel, side])
        return owner, there, (src, dst, back_recv.at[0, side])

    def forward(r):
        if r > 0:
            source = lax.rem(me + r, n)
            to_peer(
                {"ctx": source}, obuf.at[r], out.at[source], out_send.at[r], out_recv.at[r]
            ).wait_recv()
        for c in range(CORES):
            owner, there, here = hand_back(r, c)

            @pl.when(owner != mine_exp)
            def _():
                there.start()

            @pl.when(owner == mine_exp)
            def _():
                pltpu.make_async_copy(*here).start()

    for d in (4, 3, 5):
        finish(d)
    finish(0)
    forward(0)
    for d in (2, 6, 1, 7):
        finish(d)
    for r in (7, 1, 6, 2, 5, 3, 4):
        forward(r)

    def last(side, q, source):
        dst = result.at[:, lanes(source * (per_col * part) + side * part, part)]
        return to_peer(
            {"section": after, "exp": q * CORES + core},
            stage.at[side, q],
            dst,
            last_send.at[side, q],
            last_recv.at[side, source],
        )

    gate_column = gates[...].reshape(cols * tokens, 128)[:, 0:1]
    for side in range(per_col):
        for e in range(experts):
            rel = lax.rem(e - mine_exp + experts, experts)
            landed = back.at[e, :, pl.ds(side * part, part)]
            pltpu.make_async_copy(landed, landed, back_recv.at[rel, side]).wait()
        routed = lax.dot_general(
            selector[...],
            back[:, :, side * part : (side + 1) * part].reshape(experts * block_rows, part),
            (((0,), (0,)), ((), ())),
            preferred_element_type=F32,
        )
        mixture = routed * gate_column + residual[:, side * part : (side + 1) * part]
        stage[side] = mixture.astype(BF16).reshape(cols, tokens, part)
        for q in range(cols):
            last(side, q, x).start()
    for side in range(per_col):
        for q in range(cols):
            last(side, q, q).wait_recv()
    for side in range(per_col):
        for q in range(cols):
            last(side, q, x).wait_send()
    for r in range(n):
        for c in range(CORES):
            owner, there, _ = hand_back(r, c)

            @pl.when(owner != mine_exp)
            def _():
                there.wait_send()

    for copy in sent:
        copy.wait_send()


def run_experts(mine, down, residual, slots, gates, gate_shard, up_shard):
    n = lax.axis_size("ctx")
    sections = lax.axis_size("section")
    cols, tokens = gates.shape[0], gates.shape[1]
    experts = cols * CORES
    count, width = mine.shape
    units = gate_shard.shape[0]
    part = width // n
    wide = width // cols
    packed = count + count // 2
    dma = pltpu.SemaphoreType.DMA
    anywhere = pl.BlockSpec(memory_space=pl.ANY)
    in_vmem = pl.BlockSpec(memory_space=pltpu.VMEM)
    return pl.pallas_call(
        functools.partial(moe_kernel, n, sections),
        out_shape=jax.ShapeDtypeStruct((tokens, width), BF16),
        in_specs=[in_vmem] * 5 + [anywhere] * 2,
        out_specs=in_vmem,
        scratch_shapes=[
            pltpu.VMEM((n, count, part), BF16),
            pltpu.VMEM((experts, count // CORES, wide), BF16),
            pltpu.VMEM((wide // part, cols, tokens, part), BF16),
            pltpu.VMEM((experts * count // CORES, cols * tokens), BF16),
            pltpu.VMEM((n, count, width), BF16),
            pltpu.VMEM((units, width), BF16),
            pltpu.VMEM((units, width), BF16),
            pltpu.VMEM((n, n, packed, 128), BF16),
            pltpu.VMEM((n, count, part), F32),
            pltpu.VMEM((n, count, part), BF16),
            dma((2,)),
        ]
        + [dma((n // 2,))] * 8
        + [dma((n,))] * 2
        + [dma((n, CORES)), dma((experts, wide // part))]
        + [dma((wide // part, cols))] * 2,
        compiler_params=pltpu.CompilerParams(
            collective_id=0, has_side_effects=True, vmem_limit_bytes=56 * 2**20
        ),
        cost_estimate=pl.CostEstimate(
            flops=6 * n * count * width * units, bytes_accessed=6 * width * units, transcendentals=0
        ),
    )(mine, down, residual, slots, gates, gate_shard, up_shard)


def per_device(
    hidden_in,
    queries,
    keys,
    values,
    out_weight,
    norm_gain,
    w_gate,
    w_up,
    w_down_t,
    expert_ids,
    route_gates,
):
    exp_count = lax.axis_size("exp")
    tokens_here = hidden_in.shape[2]
    capacity = 5 * tokens_here // (4 * exp_count)
    ids = jnp.broadcast_to(expert_ids[0, 0].reshape(1, tokens_here), (exp_count, tokens_here))
    gates = jnp.broadcast_to(route_gates[0, 0], (tokens_here, 128))
    residual, mine, slots, gates_all, down = run_attend(
        queries[0, 0],
        jnp.concatenate([keys[0, 0], values[0, 0]], axis=1),
        ids,
        gates,
        norm_gain,
        hidden_in[0, 0],
        out_weight[0],
        w_down_t[0, 0].T,
        capacity,
    )
    moved = run_experts(
        mine.reshape(exp_count * capacity, D),
        down,
        residual,
        slots,
        gates_all,
        w_gate[0, 0].T,
        w_up[0, 0].T,
    )
    return moved.reshape(1, 1, tokens_here, D)


def solution(mesh):
    return jax.shard_map(
        per_device,
        mesh=mesh,
        in_specs=(
            P("section", "exp", "ctx", None),
            P("section", "exp", "ctx", None),
            P("section", "exp", "ctx", None),
            P("section", "exp", "ctx", None),
            P("section", "ctx", None),
            P("section", None),
            P("section", "exp", None, "ctx"),
            P("section", "exp", None, "ctx"),
            P("section", "exp", None, "ctx"),
            P("section", "exp", "ctx", None),
            P("section", "exp", "ctx", None),
        ),
        out_specs=P("section", "exp", "ctx", None),
        check_vma=False,
    )
```

```python
import functools
import math

import jax
import jax.numpy as jnp
from jax import lax
from jax.experimental import pallas as pl
from jax.experimental.pallas import tpu as pltpu
from jax.sharding import PartitionSpec as P

D = 4096
QUERY_HEADS = 32
KEY_VALUE_HEADS = 2
HEAD_SIZE = 128
CORES = 2
MESH = pl.DeviceIdType.MESH
BF16, F32, I32 = jnp.bfloat16, jnp.float32, jnp.int32


def to_peer(peer, src, dst, send_sem, recv_sem):
    return pltpu.make_async_remote_copy(
        src_ref=src,
        dst_ref=dst,
        send_sem=send_sem,
        recv_sem=recv_sem,
        device_id=peer,
        device_id_type=MESH,
    )


def greet(peers):
    barrier = pltpu.get_barrier_semaphore()
    for peer in peers:
        pl.semaphore_signal(barrier, inc=1, device_id=peer, device_id_type=MESH)
    pl.semaphore_wait(barrier, len(peers))


def lanes(start, size):
    return pl.ds(pl.multiple_of(start, 128), size)


def across(a, b):
    return lax.dot_general(a, b, (((1,), (1,)), ((), ())), preferred_element_type=F32)


def layer_kernel(
    n,
    cols,
    sections,
    capacity,
    query,
    key_in,
    value_in,
    ids_in,
    gates_in,
    gain,
    hidden_any,
    weight_any,
    gate_any,
    up_any,
    down_any,
    result,
    kv,
    mixed,
    weight,
    hidden,
    ids,
    gates,
    squares,
    bias,
    residual,
    selector,
    selector_t,
    outgoing,
    rows,
    gate,
    up,
    down,
    hid,
    acc,
    obuf,
    out,
    back,
    stage,
    local_sem,
    gate_sem,
    up_sem,
    kr_send,
    kr_recv,
    kl_send,
    kl_recv,
    wr_send,
    wr_recv,
    wl_send,
    wl_recv,
    sib_send,
    sib_recv,
    x_send,
    x_recv,
    small_send,
    small_recv,
    sq_send,
    sq_recv,
    wd_send,
    wd_recv,
    disp_send,
    disp_recv,
    rr_send,
    rr_recv,
    rl_send,
    rl_recv,
    hr_send,
    hr_recv,
    hl_send,
    hl_recv,
    out_send,
    out_recv,
    back_send,
    back_recv,
    last_send,
    last_recv,
):
    z = lax.axis_index("ctx")
    me = lax.axis_index("exp")
    section = lax.axis_index("section")
    x, core = me // CORES, lax.rem(me, CORES)
    experts = cols * CORES
    half = n // 2
    tokens, width = query.shape
    wide = width // cols
    chunk = width // n
    part = width // n
    per_col = n // cols
    heads = chunk // HEAD_SIZE
    group = QUERY_HEADS // KEY_VALUE_HEADS // heads
    streams = rows.shape[1]
    stream = wide // streams
    count = rows.shape[2]
    block_rows = count // CORES
    units = gate.shape[1]
    pair = count // 2
    piece = 128
    pieces = part // piece
    up_z, down_z = {"ctx": lax.rem(z + 1, n)}, {"ctx": lax.rem(z + n - 1, n)}
    col = [lax.rem(x + d, cols) for d in range(cols)]
    same = [{"exp": col[d] * CORES + core} for d in range(cols)]
    sibling = {"exp": x * CORES + 1 - core}
    after, before = lax.rem(section + 1, sections), lax.rem(section + sections - 1, sections)

    loads = [
        pltpu.make_async_copy(
            weight_any.at[:, lanes(x * wide, chunk)], weight.at[z, 0], local_sem.at[0]
        ),
        pltpu.make_async_copy(
            weight_any.at[:, lanes(x * wide + chunk, chunk)], weight.at[z, 1], local_sem.at[1]
        ),
        pltpu.make_async_copy(hidden_any.at[:, lanes(x * wide, wide)], hidden.at[x], local_sem.at[2]),
        pltpu.make_async_copy(down_any.at[:, lanes(z * part, part)], down.at[0], local_sem.at[3]),
    ]
    expert_loads = [
        pltpu.make_async_copy(
            src.at[:, pl.ds(q * wide + h * stream, stream)],
            dst.at[h, :, pl.ds(q * stream, stream)],
            sem.at[h, q],
        )
        for src, dst, sem in ((gate_any, gate, gate_sem), (up_any, up, up_sem))
        for h in range(streams)
        for q in range(cols)
    ]
    for copy in loads + expert_loads:
        copy.start()
    kv[z, :, 0 : key_in.shape[1]] = key_in[...]
    kv[z, :, key_in.shape[1] :] = value_in[...]
    ids[x] = jnp.broadcast_to(ids_in[...], ids.shape[1:])
    gates[x] = jnp.transpose(jnp.broadcast_to(gates_in[...], (128, tokens)))
    greet(
        [{"ctx": lax.rem(z + d, n)} for d in range(1, n)]
        + [{"exp": lax.rem(me + d, experts)} for d in range(1, experts)]
        + [{"section": at, "exp": q * CORES + core} for at in (after, before) for q in range(cols)]
    )

    def kv_step(s):
        a, b = lax.rem(z + n + 1 - s, n), lax.rem(z + s - 1, n)
        cut = tokens // 2
        one, two = kv.at[a], kv.at[b]
        if s == half:
            one, two = kv.at[a, pl.ds(0, cut)], kv.at[b, pl.ds(cut, cut)]
        return (
            to_peer(up_z, one, one, kr_send.at[s - 1], kr_recv.at[s - 1]),
            to_peer(down_z, two, two, kl_send.at[s - 1], kl_recv.at[s - 1]),
        )

    def weight_step(s):
        a, b = lax.rem(z + n + 1 - s, n), lax.rem(z + s - 1, n)
        cut = chunk // 2
        one, two = weight.at[a, core], weight.at[b, core]
        if s == half:
            one, two = weight.at[a, core, pl.ds(0, cut)], weight.at[b, core, pl.ds(cut, cut)]
        own = weight_any.at[:, lanes(x * wide + core * chunk, chunk)]
        return (
            to_peer(up_z, own if s == 1 else one, one, wr_send.at[s - 1], wr_recv.at[s - 1]),
            to_peer(down_z, own if s == 1 else two, two, wl_send.at[s - 1], wl_recv.at[s - 1]),
        )

    def share(off):
        k = lax.rem(z + off, n)
        return to_peer(
            sibling, weight.at[k, core], weight.at[k, core], sib_send.at[off], sib_recv.at[off]
        )

    def shared(off):
        k = lax.rem(z + off, n)
        return to_peer(
            sibling, weight.at[k, 1 - core], weight.at[k, 1 - core], sib_send.at[off], sib_recv.at[off]
        )

    def weight_arrived(s):
        for copy in weight_step(s):
            copy.wait_recv()
        if s < half:
            for copy in weight_step(s + 1):
                copy.start()
            share(n - s).start()
        share(s).start()

    small = []
    for d in range(1, cols):
        for at, (src, dst) in enumerate(
            (
                (ids.at[x], ids.at[x]),
                (gates.at[x], gates.at[x]),
                (hidden_any.at[:, lanes(col[d] * wide, wide)], hidden.at[x]),
            )
        ):
            small.append(
                to_peer(same[d], src, dst, small_send.at[d, at], small_recv.at[cols - d, at])
            )
    now = kv_step(1)
    for copy in now:
        copy.start()
    for copy in small:
        copy.start()

    row = lax.broadcasted_iota(I32, (tokens, n * tokens), 0) + z * tokens
    column = lax.broadcasted_iota(I32, (tokens, n * tokens), 1)
    bias[...] = jnp.where(row >= column, 0.0, -1e30)
    residual[...] = jnp.zeros_like(residual)

    for s in range(1, half + 1):
        for copy in now:
            copy.wait_recv()
        if s < half:
            now = kv_step(s + 1)
            for copy in now:
                copy.start()
    for copy in weight_step(1):
        copy.start()

    def place(j):
        odd = lax.rem(j, 2)
        off = odd * ((j + 1) // 2) + (1 - odd) * lax.rem(n - j // 2, n)
        return off, lax.rem(z + off, n)

    def chunk_first(j):
        _, k = place(j)
        return (
            to_peer(same[1], mixed.at[k, x], mixed.at[k, x], x_send.at[j, 0], x_recv.at[j, 0]),
            to_peer(same[cols - 1], mixed.at[k, x], mixed.at[k, x], x_send.at[j, 1], x_recv.at[j, 1]),
        )

    def chunk_second(j):
        _, k = place(j)
        cut = tokens // 2
        one = mixed.at[k, col[cols - 1], pl.ds(0, cut)]
        two = mixed.at[k, col[1], pl.ds(cut, cut)]
        return (
            to_peer(same[1], one, one, x_send.at[j, 2], x_recv.at[j, 2]),
            to_peer(same[cols - 1], two, two, x_send.at[j, 3], x_recv.at[j, 3]),
        )

    def chunk_forward(j):
        for copy in chunk_first(j):
            copy.wait_recv()
        for copy in chunk_second(j):
            copy.start()

    def project(j):
        off, k = place(j)
        for copy in chunk_second(j):
            copy.wait_recv()

        @pl.when(off > 0)
        def _():
            shared(off).wait_recv()

        left = mixed[k].reshape(cols * tokens, chunk)
        for side in range(CORES):
            residual[:, side * chunk : (side + 1) * chunk] += jnp.dot(
                left, weight[k, side], preferred_element_type=F32
            )

    scale = math.log2(math.e) / math.sqrt(HEAD_SIZE)

    @pl.loop(0, n)
    def _(j):
        _, k = place(j)
        kv_head = k // group
        key = kv[:, :, lanes(kv_head * HEAD_SIZE, HEAD_SIZE)].reshape(n * tokens, HEAD_SIZE)
        value = kv[
            :, :, lanes((KEY_VALUE_HEADS + kv_head) * HEAD_SIZE, HEAD_SIZE)
        ].reshape(n * tokens, HEAD_SIZE)
        for h in range(heads):
            scores = across(query[:, lanes(k * chunk + h * HEAD_SIZE, HEAD_SIZE)], key) + bias[...]
            top = jnp.max(scores, axis=-1, keepdims=True)
            shifted = jnp.exp2((scores - top) * scale)
            total = jnp.sum(shifted, axis=-1, keepdims=True)
            attended = jnp.dot(shifted.astype(BF16), value, preferred_element_type=F32)
            mixed[k, x, :, h * HEAD_SIZE : (h + 1) * HEAD_SIZE] = (attended / total).astype(BF16)
        for copy in chunk_first(j):
            copy.start()

        @pl.when(j >= 1)
        def _():
            chunk_forward(j - 1)

        @pl.when(j == 2)
        def _():
            loads[0].wait()
            loads[1].wait()
            weight_arrived(1)

        @pl.when(j == 5)
        def _():
            weight_arrived(2)

        @pl.when(j >= 3)
        def _():
            project(j - 3)

    chunk_forward(n - 1)
    weight_arrived(3)
    project(n - 3)
    project(n - 2)
    weight_arrived(4)
    downs = []
    for d in (4, 3, 5, 2, 6, 1, 7):
        peer = lax.rem(z + d, n)
        downs.append(
            to_peer(
                {"ctx": peer},
                down_any.at[:, lanes(peer * part, part)],
                down.at[n - d],
                wd_send.at[d],
                wd_recv.at[n - d],
            )
        )
        downs[-1].start()
    for copy in small:
        copy.wait_recv()
    loads[2].wait()

    expert = lax.broadcasted_iota(I32, (experts, tokens), 0)
    earlier = lax.broadcasted_iota(I32, (tokens, tokens), 0) < lax.broadcasted_iota(
        I32, (tokens, tokens), 1
    )
    earlier = jnp.where(earlier, 1.0, 0.0).astype(BF16)
    placed = []
    for q in range(cols):
        chosen = ids[q]
        named = jnp.where(expert == chosen, 1.0, 0.0)
        ahead = jnp.dot(named.astype(BF16), earlier, preferred_element_type=F32)
        rank = jnp.sum(ahead * named, axis=0, keepdims=True)
        placed.append(
            (chosen[0:1] * (cols * capacity) + q * capacity).astype(F32) + rank
        )
    placed = jnp.concatenate(placed, axis=1)
    slot = lax.broadcasted_iota(I32, selector.shape, 0).astype(F32)
    selector[...] = jnp.where(slot == placed, 1.0, 0.0).astype(BF16)
    placed_t = jnp.transpose(jnp.broadcast_to(placed, (8, cols * tokens)))[:, 0:1]
    slot = lax.broadcasted_iota(I32, selector_t.shape, 1).astype(F32)
    selector_t[...] = jnp.where(slot == placed_t, 1.0, 0.0).astype(BF16)

    project(n - 1)
    residual[...] += hidden[...].reshape(cols * tokens, wide).astype(F32)
    res = residual[...]
    squares[x] = lax.dot_general(
        jnp.ones((8, wide), F32),
        res * res,
        (((1,), (1,)), ((), ())),
        precision=lax.Precision.HIGHEST,
        preferred_element_type=F32,
    )
    sums = [
        to_peer(same[d], squares.at[x], squares.at[x], sq_send.at[d], sq_recv.at[cols - d])
        for d in range(1, cols)
    ]
    for copy in sums:
        copy.start()
    for copy in sums:
        copy.wait_recv()
    total = squares[0]
    for q in range(1, cols):
        total += squares[q]
    inverse = jnp.transpose(lax.rsqrt(total * (1.0 / width) + 1e-06))[:, 0:1]

    def rows_place(h):
        return rows.at[0, h, pl.ds(pl.multiple_of(core * block_rows, 16), block_rows), lanes(x * stream, stream)]

    def dispatch(h):
        columns = residual[:, h * stream : (h + 1) * stream]
        gains = gain[:, lanes(x * wide + h * stream, stream)].astype(F32)
        normed = (columns * inverse * gains).astype(BF16)
        picked = jnp.dot(selector[...], normed, preferred_element_type=F32).astype(BF16)
        outgoing[h] = picked.reshape(experts, block_rows, stream)
        copies = []
        for d in (4, 5, 2, 6, 3, 7, 1):
            e = lax.rem(me + d, experts)
            copies.append(
                to_peer(
                    {"exp": e},
                    outgoing.at[h, e],
                    rows_place(h),
                    disp_send.at[d, h],
                    disp_recv.at[experts - d, h],
                )
            )
            copies[-1].start()
        keep = pltpu.make_async_copy(outgoing.at[h, me], rows_place(h), disp_recv.at[0, h])
        keep.start()
        return copies, keep

    def rows_step(s, h):
        copies = []
        if s < half or h % 2 == 0:
            src, dst = rows.at[(n + 1 - s) % n, h], rows.at[n - s, h]
            copies.append(to_peer(up_z, src, dst, rr_send.at[s - 1, h], rr_recv.at[s - 1, h]))
        if s < half or h % 2 == 1:
            src, dst = rows.at[s - 1, h], rows.at[s, h]
            copies.append(to_peer(down_z, src, dst, rl_send.at[s - 1, h], rl_recv.at[s - 1, h]))
        return copies

    def expand(r):
        gate_part, up_part = 0.0, 0.0
        for h in range(streams):
            block = rows[r, h]
            gate_part += across(block, gate[h])
            up_part += across(block, up[h])
        shown = (gate_part / (1.0 + jnp.exp(-gate_part)) * up_part).astype(BF16)
        owner = lax.rem(z + r, n)
        hid[0, owner, 0:count, :] = shown[:, 0:128]
        hid[0, owner, count : count + pair, :] = jnp.concatenate(
            [shown[0:pair, 128:units], shown[pair:count, 128:units]], axis=1
        )

    dispatched = [dispatch(h) for h in range(streams)]
    sent = []
    steps = {}
    for h in range(streams):
        copies, keep = dispatched[h]
        sent += copies
        for copy in copies:
            copy.wait_recv()
        keep.wait()
        steps[1, h] = rows_step(1, h)
        for copy in steps[1, h]:
            copy.start()
    for copy in expert_loads:
        copy.wait()
    expand(0)
    for s in range(1, half + 1):
        for h in range(streams):
            for copy in steps[s, h]:
                copy.wait_recv()
            if s < half:
                steps[s + 1, h] = rows_step(s + 1, h)
                for copy in steps[s + 1, h]:
                    copy.start()
        expand(s)
        if s < half:
            expand(n - s)
    for copies in steps.values():
        sent += copies

    def hid_step(s):
        one, two = hid.at[(n + 1 - s) % n], hid.at[s - 1]
        here, there = hid.at[n - s], hid.at[s]
        if s == half:
            one, here = one.at[pl.ds(0, half)], here.at[pl.ds(0, half)]
            two, there = two.at[pl.ds(half, half)], there.at[pl.ds(half, half)]
        return (
            to_peer(up_z, one, here, hr_send.at[s - 1], hr_recv.at[s - 1]),
            to_peer(down_z, two, there, hl_send.at[s - 1], hl_recv.at[s - 1]),
        )

    def unpack(r, b):
        packed = hid[r, b]
        end = packed[count : count + pair]
        rest = jnp.concatenate([end[:, 0 : units - 128], end[:, units - 128 :]], axis=0)
        return jnp.concatenate([packed[0:count], rest], axis=1)

    def shrink(r, b):
        return jnp.dot(unpack(r, b), down[r], preferred_element_type=F32)

    now = hid_step(1)
    sent += now
    for copy in now:
        copy.start()
    loads[3].wait()
    for copy in downs:
        copy.wait_recv()

    @pl.loop(0, n)
    def _(b):
        acc[b] = shrink(0, b)

    for s in range(1, half):
        for copy in now:
            copy.wait_recv()
        now = hid_step(s + 1)
        sent += now
        for copy in now:
            copy.start()

        @pl.loop(0, n)
        def _(b):
            acc[b] += shrink(s, b) + shrink(n - s, b)

    for copy in now:
        copy.wait_recv()

    def leave(d, i):
        b = lax.rem(z + d, n)
        window = lanes(i * piece, piece)
        return to_peer(
            {"ctx": b},
            obuf.at[d, :, window],
            out.at[z, :, window],
            out_send.at[d, i],
            out_recv.at[n - d, i],
        )

    def finish(i):
        window = lanes(i * piece, piece)
        for d in (4, 3, 5, 2, 6, 1, 7, 0):
            b = lax.rem(z + d, n)
            block = acc[b, :, window] + jnp.dot(
                unpack(half, b), down[half, :, window], preferred_element_type=F32
            )
            if d == 0:
                out[z, :, window] = block.astype(BF16)
            else:
                obuf[d, :, window] = block.astype(BF16)
                leave(d, i).start()

    def hand_back(r, c, i):
        source = lax.rem(z + r, n)
        owner = source // per_col * CORES + c
        side = lax.rem(source, per_col)
        rel = lax.rem(me - owner + experts, experts)
        src = out.at[source, pl.ds(c * block_rows, block_rows), lanes(i * piece, piece)]
        dst = back.at[me, :, lanes(side * part + i * piece, piece)]
        there = to_peer({"exp": owner}, src, dst, back_send.at[r, c, i], back_recv.at[rel, side, i])
        return owner, there, (src, dst, back_recv.at[0, side, i])

    def forward(i):
        for r in (0, 7, 1, 6, 2, 5, 3, 4):
            if r > 0:
                source = lax.rem(z + r, n)
                landed = out.at[source, :, lanes(i * piece, piece)]
                pltpu.make_async_copy(landed, landed, out_recv.at[r, i]).wait()
            for c in range(CORES):
                owner, there, here = hand_back(r, c, i)

                @pl.when(owner != me)
                def _():
                    there.start()

                @pl.when(owner == me)
                def _():
                    pltpu.make_async_copy(*here).start()

    def last(side, q, source, i):
        dst = result.at[:, lanes(source * wide + side * part + i * piece, piece)]
        return to_peer(
            {"section": after, "exp": q * CORES + core},
            stage.at[i, side, q],
            dst,
            last_send.at[i, side, q],
            last_recv.at[i, side, source],
        )

    gate_column = gates[...].reshape(cols * tokens, 128)[:, 0:1]

    def combine(i):
        for side in range(per_col):
            window = lanes(side * part + i * piece, piece)
            for e in range(experts):
                rel = lax.rem(e - me + experts, experts)
                landed = back.at[e, :, window]
                pltpu.make_async_copy(landed, landed, back_recv.at[rel, side, i]).wait()
            routed = jnp.dot(
                selector_t[...],
                back[:, :, window].reshape(experts * block_rows, piece),
                preferred_element_type=F32,
            )
            mixture = routed * gate_column + residual[:, window]
            stage[i, side] = mixture.astype(BF16).reshape(cols, tokens, piece)
            for q in range(cols):
                last(side, q, x, i).start()

    @pl.loop(0, pieces + 2)
    def _(t):
        @pl.when(t < pieces)
        def _():
            finish(t)

        @pl.when((t >= 1) & (t < pieces + 1))
        def _():
            forward(t - 1)

        @pl.when(t >= 2)
        def _():
            combine(t - 2)

    @pl.loop(0, pieces)
    def _(i):
        for side in range(per_col):
            for q in range(cols):
                last(side, q, q, i).wait_recv()
                last(side, q, x, i).wait_send()
        for r in range(n):
            if r > 0:
                leave(r, i).wait_send()
            for c in range(CORES):
                owner, there, _ = hand_back(r, c, i)

                @pl.when(owner != me)
                def _():
                    there.wait_send()

    for copy in small + sums + sent + downs:
        copy.wait_send()
    for s in range(1, half + 1):
        for copy in kv_step(s) + weight_step(s):
            copy.wait_send()
    for off in range(1, n):
        share(off).wait_send()

    @pl.loop(0, n)
    def _(j):
        for copy in chunk_first(j) + chunk_second(j):
            copy.wait_send()


def run_layer(query, key, value, ids, gates, gain, hidden, weight, gate, up, down):
    n = lax.axis_size("ctx")
    experts = lax.axis_size("exp")
    sections = lax.axis_size("section")
    cols = experts // CORES
    tokens, width = query.shape
    wide, part = width // cols, width // n
    units = down.shape[0]
    capacity = 5 * tokens // (4 * experts)
    count = experts * capacity
    packed = count + count // 2
    streams = 2
    pieces = part // 128
    dma = pltpu.SemaphoreType.DMA
    anywhere = pl.BlockSpec(memory_space=pl.ANY)
    in_vmem = pl.BlockSpec(memory_space=pltpu.VMEM)
    ring = [dma((n // 2,))] * 4
    return pl.pallas_call(
        functools.partial(layer_kernel, n, cols, sections, capacity),
        out_shape=jax.ShapeDtypeStruct((tokens, width), BF16),
        in_specs=[in_vmem] * 6 + [anywhere] * 5,
        out_specs=in_vmem,
        scratch_shapes=[
            pltpu.VMEM((n, tokens, 2 * key.shape[1]), BF16),
            pltpu.VMEM((n, cols, tokens, part), BF16),
            pltpu.VMEM((n, CORES, part, part), BF16),
            pltpu.VMEM((cols, tokens, wide), BF16),
            pltpu.VMEM((cols, experts, tokens), I32),
            pltpu.VMEM((cols, tokens, 128), F32),
            pltpu.VMEM((cols, 8, cols * tokens), F32),
            pltpu.VMEM((tokens, n * tokens), F32),
            pltpu.VMEM((cols * tokens, wide), F32),
            pltpu.VMEM((experts * cols * capacity, cols * tokens), BF16),
            pltpu.VMEM((cols * tokens, experts * cols * capacity), BF16),
            pltpu.VMEM((streams, experts, count // CORES, wide // streams), BF16),
            pltpu.VMEM((n, streams, count, width // streams), BF16),
            pltpu.VMEM((streams, units, width // streams), BF16),
            pltpu.VMEM((streams, units, width // streams), BF16),
            pltpu.VMEM((n, units, part), BF16),
            pltpu.VMEM((n, n, packed, 128), BF16),
            pltpu.VMEM((n, count, part), F32),
            pltpu.VMEM((n, count, part), BF16),
            pltpu.VMEM((n, count, part), BF16),
            pltpu.VMEM((experts, count // CORES, wide), BF16),
            pltpu.VMEM((pieces, wide // part, cols, tokens, 128), BF16),
            dma((4,)),
            dma((streams, cols)),
            dma((streams, cols)),
        ]
        + ring
        + ring
        + [dma((n,))] * 2
        + [dma((n, 4))] * 2
        + [dma((cols, 3))] * 2
        + [dma((cols,))] * 2
        + [dma((n,))] * 2
        + [dma((experts, streams))] * 2
        + [dma((n // 2, streams))] * 4
        + ring
        + [dma((n, pieces))] * 2
        + [dma((n, CORES, pieces)), dma((experts, wide // part, pieces))]
        + [dma((pieces, wide // part, cols))] * 2,
        compiler_params=pltpu.CompilerParams(
            collective_id=0, has_side_effects=True, vmem_limit_bytes=60 * 2**20
        ),
        cost_estimate=pl.CostEstimate(
            flops=2 * cols * tokens * width * wide + 6 * n * count * width * units,
            bytes_accessed=16 * 2**20,
            transcendentals=QUERY_HEADS * tokens * n * tokens,
        ),
    )(query, key, value, ids, gates, gain, hidden, weight, gate, up, down)


def per_device(
    hidden_in,
    queries,
    keys,
    values,
    out_weight,
    norm_gain,
    w_gate,
    w_up,
    w_down_t,
    expert_ids,
    route_gates,
):
    tokens_here = hidden_in.shape[2]
    moved = run_layer(
        queries[0, 0],
        keys[0, 0],
        values[0, 0],
        expert_ids[0, 0].reshape(1, tokens_here),
        route_gates[0, 0].reshape(1, tokens_here),
        norm_gain,
        hidden_in[0, 0],
        out_weight[0],
        w_gate[0, 0].T,
        w_up[0, 0].T,
        w_down_t[0, 0].T,
    )
    return moved.reshape(1, 1, tokens_here, D)


def solution(mesh):
    return jax.shard_map(
        per_device,
        mesh=mesh,
        in_specs=(
            P("section", "exp", "ctx", None),
            P("section", "exp", "ctx", None),
            P("section", "exp", "ctx", None),
            P("section", "exp", "ctx", None),
            P("section", "ctx", None),
            P("section", None),
            P("section", "exp", None, "ctx"),
            P("section", "exp", None, "ctx"),
            P("section", "exp", None, "ctx"),
            P("section", "exp", "ctx", None),
            P("section", "exp", "ctx", None),
        ),
        out_specs=P("section", "exp", "ctx", None),
        check_vma=False,
    )
```

```python
import functools
import math

import jax
import jax.numpy as jnp
from jax import lax
from jax.experimental import pallas as pl
from jax.experimental.pallas import tpu as pltpu
from jax.sharding import PartitionSpec as P

D = 4096
QUERY_HEADS = 32
KEY_VALUE_HEADS = 2
HEAD_SIZE = 128
CORES = 2
MESH = pl.DeviceIdType.MESH
BF16, F32, I32 = jnp.bfloat16, jnp.float32, jnp.int32


def to_peer(peer, src, dst, send_sem, recv_sem):
    return pltpu.make_async_remote_copy(
        src_ref=src,
        dst_ref=dst,
        send_sem=send_sem,
        recv_sem=recv_sem,
        device_id=peer,
        device_id_type=MESH,
    )


def greet(peers):
    barrier = pltpu.get_barrier_semaphore()
    for peer in peers:
        pl.semaphore_signal(barrier, inc=1, device_id=peer, device_id_type=MESH)
    pl.semaphore_wait(barrier, len(peers))


def lanes(start, size):
    return pl.ds(pl.multiple_of(start, 128), size)


def across(a, b):
    return lax.dot_general(a, b, (((1,), (1,)), ((), ())), preferred_element_type=F32)


def layer_kernel(
    n,
    cols,
    sections,
    capacity,
    query_any,
    key_any,
    value_any,
    ids_any,
    gates_any,
    gain_any,
    hidden_any,
    weight_any,
    gate_any,
    up_any,
    down_any,
    result,
    query,
    ids_in,
    gates_in,
    gain,
    kv,
    mixed,
    weight,
    hidden,
    ids,
    gates,
    squares,
    bias,
    residual,
    selector,
    selector_t,
    outgoing,
    rows,
    gate,
    up,
    down,
    hid,
    acc,
    obuf,
    out,
    back,
    stage,
    local_sem,
    gate_sem,
    up_sem,
    kr_send,
    kr_recv,
    kl_send,
    kl_recv,
    wr_send,
    wr_recv,
    wl_send,
    wl_recv,
    sib_send,
    sib_recv,
    x_send,
    x_recv,
    small_send,
    small_recv,
    sq_send,
    sq_recv,
    wd_send,
    wd_recv,
    disp_send,
    disp_recv,
    rr_send,
    rr_recv,
    rl_send,
    rl_recv,
    hr_send,
    hr_recv,
    hl_send,
    hl_recv,
    out_send,
    out_recv,
    back_send,
    back_recv,
    last_send,
    last_recv,
):
    z = lax.axis_index("ctx")
    me = lax.axis_index("exp")
    section = lax.axis_index("section")
    x, core = me // CORES, lax.rem(me, CORES)
    experts = cols * CORES
    half = n // 2
    tokens, width = query.shape
    wide = width // cols
    chunk = width // n
    part = width // n
    per_col = n // cols
    heads = chunk // HEAD_SIZE
    group = QUERY_HEADS // KEY_VALUE_HEADS // heads
    streams = rows.shape[1]
    stream = wide // streams
    count = rows.shape[2]
    block_rows = count // CORES
    units = gate.shape[1]
    pair = count // 2
    piece = 128
    pieces = part // piece
    up_z, down_z = {"ctx": lax.rem(z + 1, n)}, {"ctx": lax.rem(z + n - 1, n)}
    col = [lax.rem(x + d, cols) for d in range(cols)]
    same = [{"exp": col[d] * CORES + core} for d in range(cols)]
    sibling = {"exp": x * CORES + 1 - core}
    after, before = lax.rem(section + 1, sections), lax.rem(section + sections - 1, sections)

    loads = [
        pltpu.make_async_copy(
            weight_any.at[:, lanes(x * wide, chunk)], weight.at[z, 0], local_sem.at[0]
        ),
        pltpu.make_async_copy(
            weight_any.at[:, lanes(x * wide + chunk, chunk)], weight.at[z, 1], local_sem.at[1]
        ),
        pltpu.make_async_copy(hidden_any.at[:, lanes(x * wide, wide)], hidden.at[x], local_sem.at[2]),
        pltpu.make_async_copy(down_any.at[:, lanes(z * part, part)], down.at[0], local_sem.at[3]),
        pltpu.make_async_copy(query_any, query, local_sem.at[4]),
        pltpu.make_async_copy(gain_any, gain, local_sem.at[5]),
    ]
    kv_width = key_any.shape[1]
    first_loads = [
        pltpu.make_async_copy(key_any, kv.at[z, :, pl.ds(0, kv_width)], local_sem.at[6]),
        pltpu.make_async_copy(value_any, kv.at[z, :, pl.ds(kv_width, kv_width)], local_sem.at[7]),
        pltpu.make_async_copy(ids_any, ids_in, local_sem.at[8]),
        pltpu.make_async_copy(gates_any, gates_in, local_sem.at[9]),
    ]
    expert_loads = [
        pltpu.make_async_copy(
            src.at[:, pl.ds(q * wide + h * stream, stream)],
            dst.at[h, :, pl.ds(q * stream, stream)],
            sem.at[h, q],
        )
        for src, dst, sem in ((gate_any, gate, gate_sem), (up_any, up, up_sem))
        for h in range(streams)
        for q in range(cols)
    ]
    for copy in first_loads + loads + expert_loads:
        copy.start()
    for copy in first_loads:
        copy.wait()
    ids[x] = jnp.broadcast_to(ids_in[...], ids.shape[1:])
    gates[x] = jnp.transpose(jnp.broadcast_to(gates_in[...], (128, tokens)))
    greet(
        [{"ctx": lax.rem(z + d, n)} for d in range(1, n)]
        + [{"exp": lax.rem(me + d, experts)} for d in range(1, experts)]
        + [{"section": at, "exp": q * CORES + core} for at in (after, before) for q in range(cols)]
    )

    def ring_pieces(s, h, place_up, place_down, sems):
        up_send, up_recv, down_send, down_recv = sems
        copies = []
        if s < half or h % 2 == 0:
            src, dst = place_up
            copies.append(to_peer(up_z, src, dst, up_send.at[s - 1, h], up_recv.at[s - 1, h]))
        if s < half or h % 2 == 1:
            src, dst = place_down
            copies.append(to_peer(down_z, src, dst, down_send.at[s - 1, h], down_recv.at[s - 1, h]))
        return copies

    kv_pieces, weight_pieces = kr_send.shape[1], wr_send.shape[1]

    def kv_step(s, h):
        a, b = lax.rem(z + n + 1 - s, n), lax.rem(z + s - 1, n)
        size = tokens // kv_pieces
        one, two = kv.at[a, pl.ds(h * size, size)], kv.at[b, pl.ds(h * size, size)]
        return ring_pieces(s, h, (one, one), (two, two), (kr_send, kr_recv, kl_send, kl_recv))

    def weight_step(s, h):
        a, b = lax.rem(z + n + 1 - s, n), lax.rem(z + s - 1, n)
        size = chunk // weight_pieces
        window = pl.ds(h * size, size)
        one, two = weight.at[a, core, window], weight.at[b, core, window]
        own = weight_any.at[window, lanes(x * wide + core * chunk, chunk)]
        return ring_pieces(
            s,
            h,
            (own if s == 1 else one, one),
            (own if s == 1 else two, two),
            (wr_send, wr_recv, wl_send, wl_recv),
        )

    def share(off, h, side):
        k = lax.rem(z + off, n)
        size = chunk // weight_pieces
        block = weight.at[k, side, pl.ds(h * size, size)]
        return to_peer(sibling, block, block, sib_send.at[off, h], sib_recv.at[off, h])

    def weight_arrived(s, h):
        for copy in weight_step(s, h):
            copy.wait_recv()
        if s < half:
            for copy in weight_step(s + 1, h):
                copy.start()
            share(n - s, h, core).start()
        share(s, h, core).start()

    small = []
    for d in range(1, cols):
        for at, (src, dst) in enumerate(
            (
                (ids.at[x], ids.at[x]),
                (gates.at[x], gates.at[x]),
                (hidden_any.at[:, lanes(col[d] * wide, wide)], hidden.at[x]),
            )
        ):
            small.append(
                to_peer(same[d], src, dst, small_send.at[d, at], small_recv.at[cols - d, at])
            )
    for h in range(kv_pieces):
        for copy in kv_step(1, h):
            copy.start()
    for copy in small:
        copy.start()

    row = lax.broadcasted_iota(I32, (tokens, n * tokens), 0) + z * tokens
    column = lax.broadcasted_iota(I32, (tokens, n * tokens), 1)
    bias[...] = jnp.where(row >= column, 0.0, -1e30)
    residual[...] = jnp.zeros_like(residual)

    acc[...] = jnp.zeros_like(acc)
    for s in range(1, half + 1):
        for h in range(kv_pieces):
            for copy in kv_step(s, h):
                copy.wait_recv()
            if s < half:
                for copy in kv_step(s + 1, h):
                    copy.start()
        for at, h in ((1,0),(2,1),(3,2),(3,3)):
            if s == at:
                for copy in weight_step(1, h):
                    copy.start()
    loads[4].wait()

    def place(j):
        odd = lax.rem(j, 2)
        off = odd * ((j + 1) // 2) + (1 - odd) * lax.rem(n - j // 2, n)
        return off, lax.rem(z + off, n)

    def chunk_first(j):
        _, k = place(j)
        return (
            to_peer(same[1], mixed.at[k, x], mixed.at[k, x], x_send.at[j, 0], x_recv.at[j, 0]),
            to_peer(same[cols - 1], mixed.at[k, x], mixed.at[k, x], x_send.at[j, 1], x_recv.at[j, 1]),
        )

    def chunk_second(j):
        _, k = place(j)
        cut = tokens // 2
        one = mixed.at[k, col[cols - 1], pl.ds(0, cut)]
        two = mixed.at[k, col[1], pl.ds(cut, cut)]
        return (
            to_peer(same[1], one, one, x_send.at[j, 2], x_recv.at[j, 2]),
            to_peer(same[cols - 1], two, two, x_send.at[j, 3], x_recv.at[j, 3]),
        )

    def chunk_forward(j):
        for copy in chunk_first(j):
            copy.wait_recv()
        for copy in chunk_second(j):
            copy.start()

    def project(j):
        off, k = place(j)
        for copy in chunk_second(j):
            copy.wait_recv()

        @pl.when(off > 0)
        def _():
            for h in range(weight_pieces):
                share(off, h, 1 - core).wait_recv()

        left = mixed[k].reshape(cols * tokens, chunk)
        for side in range(CORES):
            residual[:, side * chunk : (side + 1) * chunk] += jnp.dot(
                left, weight[k, side], preferred_element_type=F32
            )

    scale = math.log2(math.e) / math.sqrt(HEAD_SIZE)

    @pl.loop(0, n)
    def _(j):
        _, k = place(j)
        kv_head = k // group
        key = kv[:, :, lanes(kv_head * HEAD_SIZE, HEAD_SIZE)].reshape(n * tokens, HEAD_SIZE)
        value = kv[
            :, :, lanes((KEY_VALUE_HEADS + kv_head) * HEAD_SIZE, HEAD_SIZE)
        ].reshape(n * tokens, HEAD_SIZE)
        for h in range(heads):
            scores = across(query[:, lanes(k * chunk + h * HEAD_SIZE, HEAD_SIZE)], key) + bias[...]
            top = jnp.max(scores, axis=-1, keepdims=True)
            shifted = jnp.exp2((scores - top) * scale)
            total = jnp.sum(shifted, axis=-1, keepdims=True)
            attended = jnp.dot(shifted.astype(BF16), value, preferred_element_type=F32)
            mixed[k, x, :, h * HEAD_SIZE : (h + 1) * HEAD_SIZE] = (attended / total).astype(BF16)
        for copy in chunk_first(j):
            copy.start()

        @pl.when(j >= 1)
        def _():
            chunk_forward(j - 1)

        @pl.when(j == 1)
        def _():
            loads[0].wait()
            loads[1].wait()

        for at, (s, h) in ((0, (1, 0)), (1, (1, 1)), (1, (1, 2)), (2, (1, 3)), (3, (2, 0)), (3, (2, 1)), (4, (2, 2)), (5, (2, 3)), (6, (3, 0)), (6, (3, 1)), (7, (3, 2)), (7, (3, 3))):

            @pl.when(j == at)
            def _():
                weight_arrived(s, h)

        @pl.when(j >= 3)
        def _():
            project(j - 3)

    chunk_forward(n - 1)
    project(n - 3)
    project(n - 2)
    for h in range(weight_pieces):
        weight_arrived(half, h)
    downs = []
    for d in (4, 3, 5, 2, 6, 1, 7):
        peer = lax.rem(z + d, n)
        downs.append(
            to_peer(
                {"ctx": peer},
                down_any.at[:, lanes(peer * part, part)],
                down.at[n - d],
                wd_send.at[d],
                wd_recv.at[n - d],
            )
        )
        downs[-1].start()
    for copy in small:
        copy.wait_recv()
    loads[2].wait()
    loads[5].wait()

    expert = lax.broadcasted_iota(I32, (experts, tokens), 0)
    earlier = lax.broadcasted_iota(I32, (tokens, tokens), 0) < lax.broadcasted_iota(
        I32, (tokens, tokens), 1
    )
    earlier = jnp.where(earlier, 1.0, 0.0).astype(BF16)
    placed = []
    for q in range(cols):
        chosen = ids[q]
        named = jnp.where(expert == chosen, 1.0, 0.0)
        ahead = jnp.dot(named.astype(BF16), earlier, preferred_element_type=F32)
        rank = jnp.sum(ahead * named, axis=0, keepdims=True)
        placed.append(
            (chosen[0:1] * (cols * capacity) + q * capacity).astype(F32) + rank
        )
    placed = jnp.concatenate(placed, axis=1)
    slot = lax.broadcasted_iota(I32, selector.shape, 0).astype(F32)
    selector[...] = jnp.where(slot == placed, 1.0, 0.0).astype(BF16)
    placed_t = jnp.transpose(jnp.broadcast_to(placed, (8, cols * tokens)))[:, 0:1]
    slot = lax.broadcasted_iota(I32, selector_t.shape, 1).astype(F32)
    selector_t[...] = jnp.where(slot == placed_t, 1.0, 0.0).astype(BF16)

    project(n - 1)
    residual[...] += hidden[...].reshape(cols * tokens, wide).astype(F32)
    res = residual[...]
    squares[x] = lax.dot_general(
        jnp.ones((8, wide), F32),
        res * res,
        (((1,), (1,)), ((), ())),
        precision=lax.Precision.HIGHEST,
        preferred_element_type=F32,
    )
    sums = [
        to_peer(same[d], squares.at[x], squares.at[x], sq_send.at[d], sq_recv.at[cols - d])
        for d in range(1, cols)
    ]
    for copy in sums:
        copy.start()
    for copy in sums:
        copy.wait_recv()
    total = squares[0]
    for q in range(1, cols):
        total += squares[q]
    inverse = jnp.transpose(lax.rsqrt(total * (1.0 / width) + 1e-06))[:, 0:1]

    def rows_place(h):
        return rows.at[0, h, pl.ds(pl.multiple_of(core * block_rows, 16), block_rows), lanes(x * stream, stream)]

    def dispatch(h):
        columns = residual[:, h * stream : (h + 1) * stream]
        gains = gain[:, lanes(x * wide + h * stream, stream)].astype(F32)
        normed = (columns * inverse * gains).astype(BF16)
        picked = jnp.dot(selector[...], normed, preferred_element_type=F32).astype(BF16)
        outgoing[h] = picked.reshape(experts, block_rows, stream)
        copies = []
        for d in (4, 5, 2, 6, 3, 7, 1):
            e = lax.rem(me + d, experts)
            copies.append(
                to_peer(
                    {"exp": e},
                    outgoing.at[h, e],
                    rows_place(h),
                    disp_send.at[d, h],
                    disp_recv.at[experts - d, h],
                )
            )
            copies[-1].start()
        keep = pltpu.make_async_copy(outgoing.at[h, me], rows_place(h), disp_recv.at[0, h])
        keep.start()
        return copies, keep

    def rows_step(s, h):
        copies = []
        if s < half or h % 2 == 0:
            src, dst = rows.at[(n + 1 - s) % n, h], rows.at[n - s, h]
            copies.append(to_peer(up_z, src, dst, rr_send.at[s - 1, h], rr_recv.at[s - 1, h]))
        if s < half or h % 2 == 1:
            src, dst = rows.at[s - 1, h], rows.at[s, h]
            copies.append(to_peer(down_z, src, dst, rl_send.at[s - 1, h], rl_recv.at[s - 1, h]))
        return copies

    order = [0, 1, 7, 2, 6, 3, 5, 4]
    ready = [order.index(r) for r in range(n)]
    bounds = ((0, 3), (3, 7), (7, 8))

    def hid_step(part_at, s):
        first, end = bounds[part_at]
        blocks = pl.ds(first, end - first)
        one, here = hid.at[(n + 1 - s) % n, blocks], hid.at[n - s, blocks]
        two, there = hid.at[s - 1, blocks], hid.at[s, blocks]
        if s == half:
            cut = 128
            one, here = one.at[:, pl.ds(0, cut)], here.at[:, pl.ds(0, cut)]
            two, there = two.at[:, pl.ds(cut, count + pair - cut)], there.at[:, pl.ds(cut, count + pair - cut)]
        return (
            to_peer(up_z, one, here, hr_send.at[part_at, s - 1], hr_recv.at[part_at, s - 1]),
            to_peer(down_z, two, there, hl_send.at[part_at, s - 1], hl_recv.at[part_at, s - 1]),
        )

    def hid_start(part_at, s):
        copies = hid_step(part_at, s)
        for copy in copies:
            copy.start()
        sent.extend(copies)
        hid_now[part_at] = copies

    def hid_arrived(part_at, s):
        for copy in hid_now[part_at]:
            copy.wait_recv()
        if s < half:
            hid_start(part_at, s + 1)

    def unpack(r, p):
        packed = hid[r, p]
        end = packed[count : count + pair]
        rest = jnp.concatenate([end[:, 0 : units - 128], end[:, units - 128 :]], axis=0)
        return jnp.concatenate([packed[0:count], rest], axis=1)

    def shrink(part_at, *shards):
        @pl.loop(*bounds[part_at])
        def _(p):
            off, _ = place(p)
            for r in shards:
                acc[lax.rem(z + r + off, n)] += jnp.dot(
                    unpack(r, p), down[r], preferred_element_type=F32
                )

    def expand(r):
        gate_part, up_part = 0.0, 0.0
        for h in range(streams):
            block = rows[r, h]
            gate_part += across(block, gate[h])
            up_part += across(block, up[h])
        shown = (gate_part / (1.0 + jnp.exp(-gate_part)) * up_part).astype(BF16)
        hid[0, ready[r], 0:count, :] = shown[:, 0:128]
        hid[0, ready[r], count : count + pair, :] = jnp.concatenate(
            [shown[0:pair, 128:units], shown[pair:count, 128:units]], axis=1
        )

    dispatched = [dispatch(h) for h in range(streams)]
    sent = []
    steps = {}
    for h in range(streams):
        copies, keep = dispatched[h]
        sent += copies
        for copy in copies:
            copy.wait_recv()
        keep.wait()
        steps[1, h] = rows_step(1, h)
        for copy in steps[1, h]:
            copy.start()
        sent += steps[1, h]
    for copy in expert_loads:
        copy.wait()
    expand(0)
    hid_now = {}
    for s in range(1, half + 1):
        for h in range(streams):
            for copy in steps[s, h]:
                copy.wait_recv()
            if s < half:
                steps[s + 1, h] = rows_step(s + 1, h)
                for copy in steps[s + 1, h]:
                    copy.start()
                sent += steps[s + 1, h]
        if s > 1:
            hid_arrived(0, s - 1)
        if s < half:
            expand(s)
            expand(n - s)
        else:
            expand(half)
        if s == 1:
            hid_start(0, 1)
            loads[3].wait()
            for copy in downs:
                copy.wait_recv()
            shrink(0, 0)
        elif s == 2:
            shrink(0, 1, n - 1)
        elif s == 3:
            hid_start(1, 1)
            shrink(0, 2, n - 2)
            shrink(1, 0)
    hid_start(2, 1)
    hid_arrived(1, 1)
    shrink(0, 3, n - 3)
    shrink(1, 1, n - 1)
    hid_arrived(2, 1)
    shrink(2, 0, 1, n - 1)
    hid_arrived(1, 2)
    hid_arrived(2, 2)
    shrink(1, 2, n - 2)
    shrink(2, 2, n - 2)
    hid_arrived(1, 3)
    hid_arrived(2, 3)
    shrink(1, 3, n - 3)
    shrink(2, 3, n - 3)
    for part_at in range(len(bounds)):
        hid_arrived(part_at, half)

    def leave(d, i):
        b = lax.rem(z + d, n)
        window = lanes(i * piece, piece)
        return to_peer(
            {"ctx": b},
            obuf.at[d, :, window],
            out.at[z, :, window],
            out_send.at[d, i],
            out_recv.at[n - d, i],
        )

    def finish(i):
        window = lanes(i * piece, piece)
        for d in (4, 3, 5, 2, 6, 1, 7, 0):
            b = lax.rem(z + d, n)
            block = acc[b, :, window] + jnp.dot(
                unpack(half, ready[(d + half) % n]), down[half, :, window], preferred_element_type=F32
            )
            if d == 0:
                out[z, :, window] = block.astype(BF16)
            else:
                obuf[d, :, window] = block.astype(BF16)
                leave(d, i).start()

    def hand_back(r, c, i):
        source = lax.rem(z + r, n)
        owner = source // per_col * CORES + c
        side = lax.rem(source, per_col)
        rel = lax.rem(me - owner + experts, experts)
        src = out.at[source, pl.ds(c * block_rows, block_rows), lanes(i * piece, piece)]
        dst = back.at[me, :, lanes(side * part + i * piece, piece)]
        there = to_peer({"exp": owner}, src, dst, back_send.at[r, c, i], back_recv.at[rel, side, i])
        return owner, there, (src, dst, back_recv.at[0, side, i])

    def forward(i):
        for r in (0, 7, 1, 6, 2, 5, 3, 4):
            if r > 0:
                source = lax.rem(z + r, n)
                landed = out.at[source, :, lanes(i * piece, piece)]
                pltpu.make_async_copy(landed, landed, out_recv.at[r, i]).wait()
            for c in range(CORES):
                owner, there, here = hand_back(r, c, i)

                @pl.when(owner != me)
                def _():
                    there.start()

                @pl.when(owner == me)
                def _():
                    pltpu.make_async_copy(*here).start()

    def last(side, q, source, i):
        dst = result.at[:, lanes(source * wide + side * part + i * piece, piece)]
        return to_peer(
            {"section": after, "exp": q * CORES + core},
            stage.at[i, side, q],
            dst,
            last_send.at[i, side, q],
            last_recv.at[i, side, source],
        )

    gate_column = gates[...].reshape(cols * tokens, 128)[:, 0:1]

    def combine(i):
        for side in range(per_col):
            window = lanes(side * part + i * piece, piece)
            for e in range(experts):
                rel = lax.rem(e - me + experts, experts)
                landed = back.at[e, :, window]
                pltpu.make_async_copy(landed, landed, back_recv.at[rel, side, i]).wait()
            routed = jnp.dot(
                selector_t[...],
                back[:, :, window].reshape(experts * block_rows, piece),
                preferred_element_type=F32,
            )
            mixture = routed * gate_column + residual[:, window]
            stage[i, side] = mixture.astype(BF16).reshape(cols, tokens, piece)
            for q in range(cols):
                last(side, q, x, i).start()

    @pl.loop(0, pieces + 2)
    def _(t):
        @pl.when(t < pieces)
        def _():
            finish(t)

        @pl.when((t >= 1) & (t < pieces + 1))
        def _():
            forward(t - 1)

        @pl.when(t >= 2)
        def _():
            combine(t - 2)

    @pl.loop(0, pieces)
    def _(i):
        for side in range(per_col):
            for q in range(cols):
                last(side, q, q, i).wait_recv()
                last(side, q, x, i).wait_send()
        for r in range(n):
            if r > 0:
                leave(r, i).wait_send()
            for c in range(CORES):
                owner, there, _ = hand_back(r, c, i)

                @pl.when(owner != me)
                def _():
                    there.wait_send()

    for copy in small + sums + sent + downs:
        copy.wait_send()
    for s in range(1, half + 1):
        for h in range(kv_pieces):
            for copy in kv_step(s, h):
                copy.wait_send()
        for h in range(weight_pieces):
            for copy in weight_step(s, h):
                copy.wait_send()
    for off in range(1, n):
        for h in range(weight_pieces):
            share(off, h, core).wait_send()

    @pl.loop(0, n)
    def _(j):
        for copy in chunk_first(j) + chunk_second(j):
            copy.wait_send()


def run_layer(query, key, value, ids, gates, gain, hidden, weight, gate, up, down):
    n = lax.axis_size("ctx")
    experts = lax.axis_size("exp")
    sections = lax.axis_size("section")
    cols = experts // CORES
    tokens, width = query.shape
    wide, part = width // cols, width // n
    units = down.shape[0]
    capacity = 5 * tokens // (4 * experts)
    count = experts * capacity
    packed = count + count // 2
    streams = 2
    pieces = part // 128
    dma = pltpu.SemaphoreType.DMA
    anywhere = pl.BlockSpec(memory_space=pl.ANY)
    return pl.pallas_call(
        functools.partial(layer_kernel, n, cols, sections, capacity),
        out_shape=jax.ShapeDtypeStruct((tokens, width), BF16),
        in_specs=[anywhere] * 11,
        out_specs=anywhere,
        scratch_shapes=[
            pltpu.VMEM((tokens, width), BF16),
            pltpu.VMEM(ids.shape, I32),
            pltpu.VMEM(gates.shape, F32),
            pltpu.VMEM(gain.shape, BF16),
            pltpu.VMEM((n, tokens, 2 * key.shape[1]), BF16),
            pltpu.VMEM((n, cols, tokens, part), BF16),
            pltpu.VMEM((n, CORES, part, part), BF16),
            pltpu.VMEM((cols, tokens, wide), BF16),
            pltpu.VMEM((cols, experts, tokens), I32),
            pltpu.VMEM((cols, tokens, 128), F32),
            pltpu.VMEM((cols, 8, cols * tokens), F32),
            pltpu.VMEM((tokens, n * tokens), F32),
            pltpu.VMEM((cols * tokens, wide), F32),
            pltpu.VMEM((experts * cols * capacity, cols * tokens), BF16),
            pltpu.VMEM((cols * tokens, experts * cols * capacity), BF16),
            pltpu.VMEM((streams, experts, count // CORES, wide // streams), BF16),
            pltpu.VMEM((n, streams, count, width // streams), BF16),
            pltpu.VMEM((streams, units, width // streams), BF16),
            pltpu.VMEM((streams, units, width // streams), BF16),
            pltpu.VMEM((n, units, part), BF16),
            pltpu.VMEM((n, n, packed, 128), BF16),
            pltpu.VMEM((n, count, part), F32),
            pltpu.VMEM((n, count, part), BF16),
            pltpu.VMEM((n, count, part), BF16),
            pltpu.VMEM((experts, count // CORES, wide), BF16),
            pltpu.VMEM((pieces, wide // part, cols, tokens, 128), BF16),
            dma((10,)),
            dma((streams, cols)),
            dma((streams, cols)),
        ]
        + [dma((n // 2, 2))] * 4
        + [dma((n // 2, 4))] * 4
        + [dma((n, 4))] * 2
        + [dma((n, 4))] * 2
        + [dma((cols, 3))] * 2
        + [dma((cols,))] * 2
        + [dma((n,))] * 2
        + [dma((experts, streams))] * 2
        + [dma((n // 2, streams))] * 4
        + [dma((3, n // 2))] * 4
        + [dma((n, pieces))] * 2
        + [dma((n, CORES, pieces)), dma((experts, wide // part, pieces))]
        + [dma((pieces, wide // part, cols))] * 2,
        compiler_params=pltpu.CompilerParams(
            collective_id=0, has_side_effects=True, vmem_limit_bytes=60 * 2**20
        ),
        cost_estimate=pl.CostEstimate(
            flops=2 * cols * tokens * width * wide + 6 * n * count * width * units,
            bytes_accessed=16 * 2**20,
            transcendentals=QUERY_HEADS * tokens * n * tokens,
        ),
    )(query, key, value, ids, gates, gain, hidden, weight, gate, up, down)


def per_device(
    hidden_in,
    queries,
    keys,
    values,
    out_weight,
    norm_gain,
    w_gate,
    w_up,
    w_down_t,
    expert_ids,
    route_gates,
):
    tokens_here = hidden_in.shape[2]
    moved = run_layer(
        queries[0, 0],
        keys[0, 0],
        values[0, 0],
        expert_ids[0, 0].reshape(1, tokens_here),
        route_gates[0, 0].reshape(1, tokens_here),
        norm_gain,
        hidden_in[0, 0],
        out_weight[0],
        w_gate[0, 0].T,
        w_up[0, 0].T,
        w_down_t[0, 0].T,
    )
    return moved.reshape(1, 1, tokens_here, D)


def solution(mesh):
    return jax.shard_map(
        per_device,
        mesh=mesh,
        in_specs=(
            P("section", "exp", "ctx", None),
            P("section", "exp", "ctx", None),
            P("section", "exp", "ctx", None),
            P("section", "exp", "ctx", None),
            P("section", "ctx", None),
            P("section", None),
            P("section", "exp", None, "ctx"),
            P("section", "exp", None, "ctx"),
            P("section", "exp", None, "ctx"),
            P("section", "exp", "ctx", None),
            P("section", "exp", "ctx", None),
        ),
        out_specs=P("section", "exp", "ctx", None),
        check_vma=False,
    )
```

```python
import functools
import math

import jax
import jax.numpy as jnp
from jax import lax
from jax.experimental import pallas as pl
from jax.experimental.pallas import tpu as pltpu
from jax.sharding import PartitionSpec as P

D = 4096
QUERY_HEADS = 32
KEY_VALUE_HEADS = 2
HEAD_SIZE = 128
CORES = 2
MESH = pl.DeviceIdType.MESH
BF16, F32, I32 = jnp.bfloat16, jnp.float32, jnp.int32


def to_peer(peer, src, dst, send_sem, recv_sem):
    return pltpu.make_async_remote_copy(
        src_ref=src,
        dst_ref=dst,
        send_sem=send_sem,
        recv_sem=recv_sem,
        device_id=peer,
        device_id_type=MESH,
    )


def greet(peers):
    for peer in peers:
        pl.semaphore_signal(
            pltpu.get_barrier_semaphore(), inc=1, device_id=peer, device_id_type=MESH
        )


def greeted(peers):
    pl.semaphore_wait(pltpu.get_barrier_semaphore(), len(peers))


def lanes(start, size):
    return pl.ds(pl.multiple_of(start, 128), size)


def across(a, b):
    return lax.dot_general(a, b, (((1,), (1,)), ((), ())), preferred_element_type=F32)


def layer_kernel(
    n,
    cols,
    sections,
    capacity,
    query_any,
    key_any,
    value_any,
    ids_any,
    gates_any,
    gain_any,
    hidden_any,
    weight_any,
    gate_any,
    up_any,
    down_any,
    result,
    query,
    ids_in,
    gates_in,
    gain,
    kv,
    mixed,
    weight,
    hidden,
    ids,
    gates,
    squares,
    bias,
    residual,
    selector,
    selector_t,
    outgoing,
    rows,
    gate,
    up,
    down,
    hid,
    acc,
    obuf,
    out,
    back,
    stage,
    local_sem,
    gate_sem,
    up_sem,
    kr_send,
    kr_recv,
    kl_send,
    kl_recv,
    wr_send,
    wr_recv,
    wl_send,
    wl_recv,
    sib_send,
    sib_recv,
    x_send,
    x_recv,
    small_send,
    small_recv,
    sq_send,
    sq_recv,
    wd_send,
    wd_recv,
    disp_send,
    disp_recv,
    rr_send,
    rr_recv,
    rl_send,
    rl_recv,
    hr_send,
    hr_recv,
    hl_send,
    hl_recv,
    out_send,
    out_recv,
    back_send,
    back_recv,
    last_send,
    last_recv,
):
    z = lax.axis_index("ctx")
    me = lax.axis_index("exp")
    section = lax.axis_index("section")
    x, core = me // CORES, lax.rem(me, CORES)
    experts = cols * CORES
    half = n // 2
    tokens, width = query.shape
    wide = width // cols
    chunk = width // n
    part = width // n
    per_col = n // cols
    heads = chunk // HEAD_SIZE
    group = QUERY_HEADS // KEY_VALUE_HEADS // heads
    streams = rows.shape[1]
    stream = wide // streams
    count = rows.shape[2]
    block_rows = count // CORES
    units = gate.shape[1]
    pair = count // 2
    piece = 128
    pieces = part // piece
    up_z, down_z = {"ctx": lax.rem(z + 1, n)}, {"ctx": lax.rem(z + n - 1, n)}
    col = [lax.rem(x + d, cols) for d in range(cols)]
    same = [{"exp": col[d] * CORES + core} for d in range(cols)]
    sibling = {"exp": x * CORES + 1 - core}
    after, before = lax.rem(section + 1, sections), lax.rem(section + sections - 1, sections)

    peers = (
        [{"ctx": lax.rem(z + d, n)} for d in range(1, n)]
        + [{"exp": lax.rem(me + d, experts)} for d in range(1, experts)]
        + [{"section": at, "exp": q * CORES + core} for at in (after, before) for q in range(cols)]
    )
    greet(peers)

    loads = [
        pltpu.make_async_copy(
            weight_any.at[:, lanes(x * wide, chunk)], weight.at[z, 0], local_sem.at[0]
        ),
        pltpu.make_async_copy(
            weight_any.at[:, lanes(x * wide + chunk, chunk)], weight.at[z, 1], local_sem.at[1]
        ),
        pltpu.make_async_copy(hidden_any.at[:, lanes(x * wide, wide)], hidden.at[x], local_sem.at[2]),
        pltpu.make_async_copy(down_any.at[:, lanes(z * part, part)], down.at[0], local_sem.at[3]),
        pltpu.make_async_copy(query_any, query, local_sem.at[4]),
        pltpu.make_async_copy(gain_any, gain, local_sem.at[5]),
    ]
    kv_width = key_any.shape[1]
    first_loads = [
        pltpu.make_async_copy(key_any, kv.at[z, :, pl.ds(0, kv_width)], local_sem.at[6]),
        pltpu.make_async_copy(value_any, kv.at[z, :, pl.ds(kv_width, kv_width)], local_sem.at[7]),
        pltpu.make_async_copy(ids_any, ids_in, local_sem.at[8]),
        pltpu.make_async_copy(gates_any, gates_in, local_sem.at[9]),
    ]
    expert_loads = [
        pltpu.make_async_copy(
            src.at[:, pl.ds(q * wide + h * stream, stream)],
            dst.at[h, :, pl.ds(q * stream, stream)],
            sem.at[h, q],
        )
        for src, dst, sem in ((gate_any, gate, gate_sem), (up_any, up, up_sem))
        for h in range(streams)
        for q in range(cols)
    ]
    for copy in first_loads + loads:
        copy.start()
    for copy in first_loads:
        copy.wait()
    ids[x] = jnp.broadcast_to(ids_in[...], ids.shape[1:])
    gates[x] = jnp.transpose(jnp.broadcast_to(gates_in[...], (128, tokens)))
    greeted(peers)

    def ring_pieces(s, h, place_up, place_down, sems):
        up_send, up_recv, down_send, down_recv = sems
        copies = []
        if s < half or h % 2 == 0:
            src, dst = place_up
            copies.append(to_peer(up_z, src, dst, up_send.at[s - 1, h], up_recv.at[s - 1, h]))
        if s < half or h % 2 == 1:
            src, dst = place_down
            copies.append(to_peer(down_z, src, dst, down_send.at[s - 1, h], down_recv.at[s - 1, h]))
        return copies

    kv_pieces, weight_pieces = kr_send.shape[1], wr_send.shape[1]

    def kv_step(s, h):
        a, b = lax.rem(z + n + 1 - s, n), lax.rem(z + s - 1, n)
        size = tokens // kv_pieces
        one, two = kv.at[a, pl.ds(h * size, size)], kv.at[b, pl.ds(h * size, size)]
        return ring_pieces(s, h, (one, one), (two, two), (kr_send, kr_recv, kl_send, kl_recv))

    def weight_step(s, h):
        a, b = lax.rem(z + n + 1 - s, n), lax.rem(z + s - 1, n)
        size = chunk // weight_pieces
        window = pl.ds(h * size, size)
        one, two = weight.at[a, core, window], weight.at[b, core, window]
        own = weight_any.at[window, lanes(x * wide + core * chunk, chunk)]
        return ring_pieces(
            s,
            h,
            (own if s == 1 else one, one),
            (own if s == 1 else two, two),
            (wr_send, wr_recv, wl_send, wl_recv),
        )

    def share(off, h, side):
        k = lax.rem(z + off, n)
        size = chunk // weight_pieces
        block = weight.at[k, side, pl.ds(h * size, size)]
        return to_peer(sibling, block, block, sib_send.at[off, h], sib_recv.at[off, h])

    def weight_arrived(s, h):
        for copy in weight_step(s, h):
            copy.wait_recv()
        if s < half:
            for copy in weight_step(s + 1, h):
                copy.start()
            share(n - s, h, core).start()
        share(s, h, core).start()

    small = []
    for d in range(1, cols):
        for at, (src, dst) in enumerate(
            (
                (ids.at[x], ids.at[x]),
                (gates.at[x], gates.at[x]),
                (hidden_any.at[:, lanes(col[d] * wide, wide)], hidden.at[x]),
            )
        ):
            small.append(
                to_peer(same[d], src, dst, small_send.at[d, at], small_recv.at[cols - d, at])
            )
    for h in range(kv_pieces):
        for copy in kv_step(1, h):
            copy.start()
    for copy in small + expert_loads:
        copy.start()

    row = lax.broadcasted_iota(I32, (tokens, n * tokens), 0) + z * tokens
    column = lax.broadcasted_iota(I32, (tokens, n * tokens), 1)
    bias[...] = jnp.where(row >= column, 0.0, -1e30)
    residual[...] = jnp.zeros_like(residual)

    acc[...] = jnp.zeros_like(acc)
    for s in range(1, half + 1):
        for h in range(kv_pieces):
            for copy in kv_step(s, h):
                copy.wait_recv()
            if s < half:
                for copy in kv_step(s + 1, h):
                    copy.start()
        for at, h in ((1,0),(2,1),(3,2),(3,3)):
            if s == at:
                for copy in weight_step(1, h):
                    copy.start()
    loads[4].wait()

    def place(j):
        odd = lax.rem(j, 2)
        off = odd * ((j + 1) // 2) + (1 - odd) * lax.rem(n - j // 2, n)
        return off, lax.rem(z + off, n)

    def chunk_first(j):
        _, k = place(j)
        return (
            to_peer(same[1], mixed.at[k, x], mixed.at[k, x], x_send.at[j, 0], x_recv.at[j, 0]),
            to_peer(same[cols - 1], mixed.at[k, x], mixed.at[k, x], x_send.at[j, 1], x_recv.at[j, 1]),
        )

    def chunk_second(j):
        _, k = place(j)
        cut = tokens // 2
        one = mixed.at[k, col[cols - 1], pl.ds(0, cut)]
        two = mixed.at[k, col[1], pl.ds(cut, cut)]
        return (
            to_peer(same[1], one, one, x_send.at[j, 2], x_recv.at[j, 2]),
            to_peer(same[cols - 1], two, two, x_send.at[j, 3], x_recv.at[j, 3]),
        )

    def chunk_forward(j):
        for copy in chunk_first(j):
            copy.wait_recv()
        for copy in chunk_second(j):
            copy.start()

    def project(j):
        off, k = place(j)
        for copy in chunk_second(j):
            copy.wait_recv()

        @pl.when(off > 0)
        def _():
            for h in range(weight_pieces):
                share(off, h, 1 - core).wait_recv()

        left = mixed[k].reshape(cols * tokens, chunk)
        for side in range(CORES):
            residual[:, side * chunk : (side + 1) * chunk] += jnp.dot(
                left, weight[k, side], preferred_element_type=F32
            )

    scale = math.log2(math.e) / math.sqrt(HEAD_SIZE)

    @pl.loop(0, n)
    def _(j):
        _, k = place(j)
        kv_head = k // group
        key = kv[:, :, lanes(kv_head * HEAD_SIZE, HEAD_SIZE)].reshape(n * tokens, HEAD_SIZE)
        value = kv[
            :, :, lanes((KEY_VALUE_HEADS + kv_head) * HEAD_SIZE, HEAD_SIZE)
        ].reshape(n * tokens, HEAD_SIZE)
        for h in range(heads):
            scores = across(query[:, lanes(k * chunk + h * HEAD_SIZE, HEAD_SIZE)], key) + bias[...]
            top = jnp.max(scores, axis=-1, keepdims=True)
            shifted = jnp.exp2((scores - top) * scale)
            total = jnp.sum(shifted, axis=-1, keepdims=True)
            attended = jnp.dot(shifted.astype(BF16), value, preferred_element_type=F32)
            mixed[k, x, :, h * HEAD_SIZE : (h + 1) * HEAD_SIZE] = (attended / total).astype(BF16)
        for copy in chunk_first(j):
            copy.start()

        @pl.when(j >= 1)
        def _():
            chunk_forward(j - 1)

        @pl.when(j == 1)
        def _():
            loads[0].wait()
            loads[1].wait()

        for at, (s, h) in ((0, (1, 0)), (1, (1, 1)), (1, (1, 2)), (2, (1, 3)), (3, (2, 0)), (3, (2, 1)), (4, (2, 2)), (5, (2, 3)), (6, (3, 0)), (6, (3, 1)), (7, (3, 2)), (7, (3, 3))):

            @pl.when(j == at)
            def _():
                weight_arrived(s, h)

        @pl.when(j >= 3)
        def _():
            project(j - 3)

    chunk_forward(n - 1)
    project(n - 3)
    project(n - 2)
    for h in range(weight_pieces):
        weight_arrived(half, h)
    downs = []
    for d in (4, 3, 5, 2, 6, 1, 7):
        peer = lax.rem(z + d, n)
        downs.append(
            to_peer(
                {"ctx": peer},
                down_any.at[:, lanes(peer * part, part)],
                down.at[n - d],
                wd_send.at[d],
                wd_recv.at[n - d],
            )
        )
        downs[-1].start()
    for copy in small:
        copy.wait_recv()
    loads[2].wait()
    loads[5].wait()

    expert = lax.broadcasted_iota(I32, (experts, tokens), 0)
    earlier = lax.broadcasted_iota(I32, (tokens, tokens), 0) < lax.broadcasted_iota(
        I32, (tokens, tokens), 1
    )
    earlier = jnp.where(earlier, 1.0, 0.0).astype(BF16)
    placed = []
    for q in range(cols):
        chosen = ids[q]
        named = jnp.where(expert == chosen, 1.0, 0.0)
        ahead = jnp.dot(named.astype(BF16), earlier, preferred_element_type=F32)
        rank = jnp.sum(ahead * named, axis=0, keepdims=True)
        placed.append(
            (chosen[0:1] * (cols * capacity) + q * capacity).astype(F32) + rank
        )
    placed = jnp.concatenate(placed, axis=1)
    slot = lax.broadcasted_iota(I32, selector.shape, 0).astype(F32)
    selector[...] = jnp.where(slot == placed, 1.0, 0.0).astype(BF16)
    placed_t = jnp.transpose(jnp.broadcast_to(placed, (8, cols * tokens)))[:, 0:1]
    slot = lax.broadcasted_iota(I32, selector_t.shape, 1).astype(F32)
    selector_t[...] = jnp.where(slot == placed_t, 1.0, 0.0).astype(BF16)

    project(n - 1)
    residual[...] += hidden[...].reshape(cols * tokens, wide).astype(F32)
    res = residual[...]
    squares[x] = lax.dot_general(
        jnp.ones((8, wide), F32),
        res * res,
        (((1,), (1,)), ((), ())),
        precision=lax.Precision.HIGHEST,
        preferred_element_type=F32,
    )
    sums = [
        to_peer(same[d], squares.at[x], squares.at[x], sq_send.at[d], sq_recv.at[cols - d])
        for d in range(1, cols)
    ]
    for copy in sums:
        copy.start()
    for copy in sums:
        copy.wait_recv()
    total = squares[0]
    for q in range(1, cols):
        total += squares[q]
    inverse = jnp.transpose(lax.rsqrt(total * (1.0 / width) + 1e-06))[:, 0:1]

    def rows_place(h):
        return rows.at[0, h, pl.ds(pl.multiple_of(core * block_rows, 16), block_rows), lanes(x * stream, stream)]

    def dispatch(h):
        columns = residual[:, h * stream : (h + 1) * stream]
        gains = gain[:, lanes(x * wide + h * stream, stream)].astype(F32)
        normed = (columns * inverse * gains).astype(BF16)
        picked = jnp.dot(selector[...], normed, preferred_element_type=F32).astype(BF16)
        outgoing[h] = picked.reshape(experts, block_rows, stream)
        copies = []
        for d in (4, 5, 2, 6, 3, 7, 1):
            e = lax.rem(me + d, experts)
            copies.append(
                to_peer(
                    {"exp": e},
                    outgoing.at[h, e],
                    rows_place(h),
                    disp_send.at[d, h],
                    disp_recv.at[experts - d, h],
                )
            )
            copies[-1].start()
        keep = pltpu.make_async_copy(outgoing.at[h, me], rows_place(h), disp_recv.at[0, h])
        keep.start()
        return copies, keep

    def rows_step(s, h):
        copies = []
        if s < half or h % 2 == 0:
            src, dst = rows.at[(n + 1 - s) % n, h], rows.at[n - s, h]
            copies.append(to_peer(up_z, src, dst, rr_send.at[s - 1, h], rr_recv.at[s - 1, h]))
        if s < half or h % 2 == 1:
            src, dst = rows.at[s - 1, h], rows.at[s, h]
            copies.append(to_peer(down_z, src, dst, rl_send.at[s - 1, h], rl_recv.at[s - 1, h]))
        return copies

    order = [0, 1, 7, 2, 6, 3, 5, 4]
    ready = [order.index(r) for r in range(n)]
    bounds = ((0, 3), (3, 7), (7, 8))

    def hid_step(part_at, s):
        first, end = bounds[part_at]
        blocks = pl.ds(first, end - first)
        one, here = hid.at[(n + 1 - s) % n, blocks], hid.at[n - s, blocks]
        two, there = hid.at[s - 1, blocks], hid.at[s, blocks]
        if s == half:
            cut = 128
            one, here = one.at[:, pl.ds(0, cut)], here.at[:, pl.ds(0, cut)]
            two, there = two.at[:, pl.ds(cut, count + pair - cut)], there.at[:, pl.ds(cut, count + pair - cut)]
        return (
            to_peer(up_z, one, here, hr_send.at[part_at, s - 1], hr_recv.at[part_at, s - 1]),
            to_peer(down_z, two, there, hl_send.at[part_at, s - 1], hl_recv.at[part_at, s - 1]),
        )

    def hid_start(part_at, s):
        copies = hid_step(part_at, s)
        for copy in copies:
            copy.start()
        sent.extend(copies)
        hid_now[part_at] = copies

    def hid_arrived(part_at, s):
        for copy in hid_now[part_at]:
            copy.wait_recv()
        if s < half:
            hid_start(part_at, s + 1)

    def unpack(r, p):
        packed = hid[r, p]
        end = packed[count : count + pair]
        rest = jnp.concatenate([end[:, 0 : units - 128], end[:, units - 128 :]], axis=0)
        return jnp.concatenate([packed[0:count], rest], axis=1)

    def shrink(part_at, *shards):
        @pl.loop(*bounds[part_at])
        def _(p):
            off, _ = place(p)
            for r in shards:
                acc[lax.rem(z + r + off, n)] += jnp.dot(
                    unpack(r, p), down[r], preferred_element_type=F32
                )

    def expand(r):
        gate_part, up_part = 0.0, 0.0
        for h in range(streams):
            block = rows[r, h]
            gate_part += across(block, gate[h])
            up_part += across(block, up[h])
        shown = (gate_part / (1.0 + jnp.exp(-gate_part)) * up_part).astype(BF16)
        hid[0, ready[r], 0:count, :] = shown[:, 0:128]
        hid[0, ready[r], count : count + pair, :] = jnp.concatenate(
            [shown[0:pair, 128:units], shown[pair:count, 128:units]], axis=1
        )

    dispatched = [dispatch(h) for h in range(streams)]
    sent = []
    steps = {}
    for h in range(streams):
        copies, keep = dispatched[h]
        sent += copies
        for copy in copies:
            copy.wait_recv()
        keep.wait()
        steps[1, h] = rows_step(1, h)
        for copy in steps[1, h]:
            copy.start()
        sent += steps[1, h]
    for copy in expert_loads:
        copy.wait()
    expand(0)
    hid_now = {}
    for s in range(1, half + 1):
        for h in range(streams):
            for copy in steps[s, h]:
                copy.wait_recv()
            if s < half:
                steps[s + 1, h] = rows_step(s + 1, h)
                for copy in steps[s + 1, h]:
                    copy.start()
                sent += steps[s + 1, h]
        if s > 1:
            hid_arrived(0, s - 1)
        if s < half:
            expand(s)
            expand(n - s)
        else:
            expand(half)
        if s == 1:
            hid_start(0, 1)
            loads[3].wait()
            for copy in downs:
                copy.wait_recv()
            shrink(0, 0)
        elif s == 2:
            shrink(0, 1, n - 1)
        elif s == 3:
            hid_start(1, 1)
            shrink(0, 2, n - 2)
            shrink(1, 0)
    hid_start(2, 1)
    hid_arrived(1, 1)
    shrink(0, 3, n - 3)
    shrink(1, 1, n - 1)
    hid_arrived(2, 1)
    shrink(2, 0, 1, n - 1)
    hid_arrived(1, 2)
    hid_arrived(2, 2)
    shrink(1, 2, n - 2)
    shrink(2, 2, n - 2)
    hid_arrived(1, 3)
    hid_arrived(2, 3)
    shrink(1, 3, n - 3)
    shrink(2, 3, n - 3)
    for part_at in range(len(bounds)):
        hid_arrived(part_at, half)

    def leave(d, i):
        b = lax.rem(z + d, n)
        window = lanes(i * piece, piece)
        return to_peer(
            {"ctx": b},
            obuf.at[d, :, window],
            out.at[z, :, window],
            out_send.at[d, i],
            out_recv.at[n - d, i],
        )

    def finish(i):
        window = lanes(i * piece, piece)
        for d in (4, 3, 5, 2, 6, 1, 7, 0):
            b = lax.rem(z + d, n)
            block = acc[b, :, window] + jnp.dot(
                unpack(half, ready[(d + half) % n]), down[half, :, window], preferred_element_type=F32
            )
            if d == 0:
                out[z, :, window] = block.astype(BF16)
            else:
                obuf[d, :, window] = block.astype(BF16)
                leave(d, i).start()

    def hand_back(r, c, i):
        source = lax.rem(z + r, n)
        owner = source // per_col * CORES + c
        side = lax.rem(source, per_col)
        rel = lax.rem(me - owner + experts, experts)
        src = out.at[source, pl.ds(c * block_rows, block_rows), lanes(i * piece, piece)]
        dst = back.at[me, :, lanes(side * part + i * piece, piece)]
        there = to_peer({"exp": owner}, src, dst, back_send.at[r, c, i], back_recv.at[rel, side, i])
        return owner, there, (src, dst, back_recv.at[0, side, i])

    def forward(i):
        for r in (0, 7, 1, 6, 2, 5, 3, 4):
            if r > 0:
                source = lax.rem(z + r, n)
                landed = out.at[source, :, lanes(i * piece, piece)]
                pltpu.make_async_copy(landed, landed, out_recv.at[r, i]).wait()
            for c in range(CORES):
                owner, there, here = hand_back(r, c, i)

                @pl.when(owner != me)
                def _():
                    there.start()

                @pl.when(owner == me)
                def _():
                    pltpu.make_async_copy(*here).start()

    def last(side, q, source, i):
        dst = result.at[:, lanes(source * wide + side * part + i * piece, piece)]
        return to_peer(
            {"section": after, "exp": q * CORES + core},
            stage.at[i, side, q],
            dst,
            last_send.at[i, side, q],
            last_recv.at[i, side, source],
        )

    gate_column = gates[...].reshape(cols * tokens, 128)[:, 0:1]

    def combine(i):
        for side in range(per_col):
            window = lanes(side * part + i * piece, piece)
            for e in range(experts):
                rel = lax.rem(e - me + experts, experts)
                landed = back.at[e, :, window]
                pltpu.make_async_copy(landed, landed, back_recv.at[rel, side, i]).wait()
            routed = jnp.dot(
                selector_t[...],
                back[:, :, window].reshape(experts * block_rows, piece),
                preferred_element_type=F32,
            )
            mixture = routed * gate_column + residual[:, window]
            stage[i, side] = mixture.astype(BF16).reshape(cols, tokens, piece)
            for q in range(cols):
                last(side, q, x, i).start()

    @pl.loop(0, pieces + 2)
    def _(t):
        @pl.when(t < pieces)
        def _():
            finish(t)

        @pl.when((t >= 1) & (t < pieces + 1))
        def _():
            forward(t - 1)

        @pl.when(t >= 2)
        def _():
            combine(t - 2)

    @pl.loop(0, pieces)
    def _(i):
        for side in range(per_col):
            for q in range(cols):
                last(side, q, q, i).wait_recv()
                last(side, q, x, i).wait_send()
        for r in range(n):
            if r > 0:
                leave(r, i).wait_send()
            for c in range(CORES):
                owner, there, _ = hand_back(r, c, i)

                @pl.when(owner != me)
                def _():
                    there.wait_send()

    for copy in small + sums + sent + downs:
        copy.wait_send()
    for s in range(1, half + 1):
        for h in range(kv_pieces):
            for copy in kv_step(s, h):
                copy.wait_send()
        for h in range(weight_pieces):
            for copy in weight_step(s, h):
                copy.wait_send()
    for off in range(1, n):
        for h in range(weight_pieces):
            share(off, h, core).wait_send()

    @pl.loop(0, n)
    def _(j):
        for copy in chunk_first(j) + chunk_second(j):
            copy.wait_send()


def run_layer(query, key, value, ids, gates, gain, hidden, weight, gate, up, down):
    n = lax.axis_size("ctx")
    experts = lax.axis_size("exp")
    sections = lax.axis_size("section")
    cols = experts // CORES
    tokens, width = query.shape
    wide, part = width // cols, width // n
    units = down.shape[0]
    capacity = 5 * tokens // (4 * experts)
    count = experts * capacity
    packed = count + count // 2
    streams = 2
    pieces = part // 128
    dma = pltpu.SemaphoreType.DMA
    anywhere = pl.BlockSpec(memory_space=pl.ANY)
    return pl.pallas_call(
        functools.partial(layer_kernel, n, cols, sections, capacity),
        out_shape=jax.ShapeDtypeStruct((tokens, width), BF16),
        in_specs=[anywhere] * 11,
        out_specs=anywhere,
        scratch_shapes=[
            pltpu.VMEM((tokens, width), BF16),
            pltpu.VMEM(ids.shape, I32),
            pltpu.VMEM(gates.shape, F32),
            pltpu.VMEM(gain.shape, BF16),
            pltpu.VMEM((n, tokens, 2 * key.shape[1]), BF16),
            pltpu.VMEM((n, cols, tokens, part), BF16),
            pltpu.VMEM((n, CORES, part, part), BF16),
            pltpu.VMEM((cols, tokens, wide), BF16),
            pltpu.VMEM((cols, experts, tokens), I32),
            pltpu.VMEM((cols, tokens, 128), F32),
            pltpu.VMEM((cols, 8, cols * tokens), F32),
            pltpu.VMEM((tokens, n * tokens), F32),
            pltpu.VMEM((cols * tokens, wide), F32),
            pltpu.VMEM((experts * cols * capacity, cols * tokens), BF16),
            pltpu.VMEM((cols * tokens, experts * cols * capacity), BF16),
            pltpu.VMEM((streams, experts, count // CORES, wide // streams), BF16),
            pltpu.VMEM((n, streams, count, width // streams), BF16),
            pltpu.VMEM((streams, units, width // streams), BF16),
            pltpu.VMEM((streams, units, width // streams), BF16),
            pltpu.VMEM((n, units, part), BF16),
            pltpu.VMEM((n, n, packed, 128), BF16),
            pltpu.VMEM((n, count, part), F32),
            pltpu.VMEM((n, count, part), BF16),
            pltpu.VMEM((n, count, part), BF16),
            pltpu.VMEM((experts, count // CORES, wide), BF16),
            pltpu.VMEM((pieces, wide // part, cols, tokens, 128), BF16),
            dma((10,)),
            dma((streams, cols)),
            dma((streams, cols)),
        ]
        + [dma((n // 2, 2))] * 4
        + [dma((n // 2, 4))] * 4
        + [dma((n, 4))] * 2
        + [dma((n, 4))] * 2
        + [dma((cols, 3))] * 2
        + [dma((cols,))] * 2
        + [dma((n,))] * 2
        + [dma((experts, streams))] * 2
        + [dma((n // 2, streams))] * 4
        + [dma((3, n // 2))] * 4
        + [dma((n, pieces))] * 2
        + [dma((n, CORES, pieces)), dma((experts, wide // part, pieces))]
        + [dma((pieces, wide // part, cols))] * 2,
        compiler_params=pltpu.CompilerParams(
            collective_id=0, has_side_effects=True, vmem_limit_bytes=60 * 2**20
        ),
        cost_estimate=pl.CostEstimate(
            flops=2 * cols * tokens * width * wide + 6 * n * count * width * units,
            bytes_accessed=16 * 2**20,
            transcendentals=QUERY_HEADS * tokens * n * tokens,
        ),
    )(query, key, value, ids, gates, gain, hidden, weight, gate, up, down)


def per_device(
    hidden_in,
    queries,
    keys,
    values,
    out_weight,
    norm_gain,
    w_gate,
    w_up,
    w_down_t,
    expert_ids,
    route_gates,
):
    tokens_here = hidden_in.shape[2]
    moved = run_layer(
        queries[0, 0],
        keys[0, 0],
        values[0, 0],
        expert_ids[0, 0].reshape(1, tokens_here),
        route_gates[0, 0].reshape(1, tokens_here),
        norm_gain,
        hidden_in[0, 0],
        out_weight[0],
        w_gate[0, 0].T,
        w_up[0, 0].T,
        w_down_t[0, 0].T,
    )
    return moved.reshape(1, 1, tokens_here, D)


def solution(mesh):
    return jax.shard_map(
        per_device,
        mesh=mesh,
        in_specs=(
            P("section", "exp", "ctx", None),
            P("section", "exp", "ctx", None),
            P("section", "exp", "ctx", None),
            P("section", "exp", "ctx", None),
            P("section", "ctx", None),
            P("section", None),
            P("section", "exp", None, "ctx"),
            P("section", "exp", None, "ctx"),
            P("section", "exp", None, "ctx"),
            P("section", "exp", "ctx", None),
            P("section", "exp", "ctx", None),
        ),
        out_specs=P("section", "exp", "ctx", None),
        check_vma=False,
    )
```

```python
import functools
import math

import jax
import jax.numpy as jnp
from jax import lax
from jax.experimental import pallas as pl
from jax.experimental.pallas import tpu as pltpu
from jax.sharding import PartitionSpec as P

D = 4096
QUERY_HEADS = 32
KEY_VALUE_HEADS = 2
HEAD_SIZE = 128
CORES = 2
MESH = pl.DeviceIdType.MESH
BF16, F32, I32 = jnp.bfloat16, jnp.float32, jnp.int32


def to_peer(peer, src, dst, send_sem, recv_sem):
    return pltpu.make_async_remote_copy(
        src_ref=src,
        dst_ref=dst,
        send_sem=send_sem,
        recv_sem=recv_sem,
        device_id=peer,
        device_id_type=MESH,
    )


def greet(peers):
    for peer in peers:
        pl.semaphore_signal(
            pltpu.get_barrier_semaphore(), inc=1, device_id=peer, device_id_type=MESH
        )


def greeted(peers):
    pl.semaphore_wait(pltpu.get_barrier_semaphore(), len(peers))


def lanes(start, size):
    return pl.ds(pl.multiple_of(start, 128), size)


def across(a, b):
    return lax.dot_general(a, b, (((1,), (1,)), ((), ())), preferred_element_type=F32)


def layer_kernel(
    n,
    cols,
    sections,
    capacity,
    query_any,
    key_any,
    value_any,
    ids_any,
    gates_any,
    gain_any,
    hidden_any,
    weight_any,
    gate_any,
    up_any,
    down_any,
    result,
    query,
    ids_in,
    gates_in,
    gain,
    kv,
    mixed,
    weight,
    hidden,
    ids,
    gates,
    squares,
    bias,
    residual,
    selector,
    selector_t,
    outgoing,
    rows,
    gate,
    up,
    down,
    hid,
    acc,
    obuf,
    out,
    back,
    stage,
    local_sem,
    gate_sem,
    up_sem,
    kr_send,
    kr_recv,
    kl_send,
    kl_recv,
    wr_send,
    wr_recv,
    wl_send,
    wl_recv,
    sib_send,
    sib_recv,
    x_send,
    x_recv,
    small_send,
    small_recv,
    sq_send,
    sq_recv,
    wd_send,
    wd_recv,
    disp_send,
    disp_recv,
    rr_send,
    rr_recv,
    rl_send,
    rl_recv,
    hr_send,
    hr_recv,
    hl_send,
    hl_recv,
    out_send,
    out_recv,
    back_send,
    back_recv,
    last_send,
    last_recv,
):
    z = lax.axis_index("ctx")
    me = lax.axis_index("exp")
    section = lax.axis_index("section")
    x, core = me // CORES, lax.rem(me, CORES)
    experts = cols * CORES
    half = n // 2
    tokens, width = query.shape
    wide = width // cols
    chunk = width // n
    part = width // n
    per_col = n // cols
    heads = chunk // HEAD_SIZE
    group = QUERY_HEADS // KEY_VALUE_HEADS // heads
    streams = rows.shape[1]
    stream = wide // streams
    count = rows.shape[2]
    block_rows = count // CORES
    units = gate.shape[1]
    pair = count // 2
    piece = 128
    pieces = part // piece
    up_z, down_z = {"ctx": lax.rem(z + 1, n)}, {"ctx": lax.rem(z + n - 1, n)}
    col = [lax.rem(x + d, cols) for d in range(cols)]
    same = [{"exp": col[d] * CORES + core} for d in range(cols)]
    sibling = {"exp": x * CORES + 1 - core}
    after, before = lax.rem(section + 1, sections), lax.rem(section + sections - 1, sections)

    peers = (
        [{"ctx": lax.rem(z + d, n)} for d in range(1, n)]
        + [{"exp": lax.rem(me + d, experts)} for d in range(1, experts)]
        + [{"section": at, "exp": q * CORES + core} for at in (after, before) for q in range(cols)]
    )
    greet(peers)

    loads = [
        pltpu.make_async_copy(
            weight_any.at[:, lanes(x * wide, chunk)], weight.at[z, 0], local_sem.at[0]
        ),
        pltpu.make_async_copy(
            weight_any.at[:, lanes(x * wide + chunk, chunk)], weight.at[z, 1], local_sem.at[1]
        ),
        pltpu.make_async_copy(hidden_any.at[:, lanes(x * wide, wide)], hidden.at[x], local_sem.at[2]),
        pltpu.make_async_copy(down_any.at[:, lanes(z * part, part)], down.at[0], local_sem.at[3]),
        pltpu.make_async_copy(query_any, query, local_sem.at[4]),
        pltpu.make_async_copy(gain_any, gain, local_sem.at[5]),
    ]
    kv_width = key_any.shape[1]
    first_loads = [
        pltpu.make_async_copy(key_any, kv.at[z, :, pl.ds(0, kv_width)], local_sem.at[6]),
        pltpu.make_async_copy(value_any, kv.at[z, :, pl.ds(kv_width, kv_width)], local_sem.at[7]),
        pltpu.make_async_copy(ids_any, ids_in, local_sem.at[8]),
        pltpu.make_async_copy(gates_any, gates_in, local_sem.at[9]),
    ]
    expert_loads = [
        pltpu.make_async_copy(
            src.at[:, pl.ds(q * wide + h * stream, stream)],
            dst.at[h, :, pl.ds(q * stream, stream)],
            sem.at[h, q],
        )
        for src, dst, sem in ((gate_any, gate, gate_sem), (up_any, up, up_sem))
        for h in range(streams)
        for q in range(cols)
    ]
    for copy in first_loads + loads:
        copy.start()
    for copy in first_loads:
        copy.wait()
    ids[x] = jnp.broadcast_to(ids_in[...], ids.shape[1:])
    gates[x] = jnp.transpose(jnp.broadcast_to(gates_in[...], (128, tokens)))
    greeted(peers)

    def ring_pieces(s, h, place_up, place_down, sems):
        up_send, up_recv, down_send, down_recv = sems
        copies = []
        if s < half or h % 2 == 0:
            src, dst = place_up
            copies.append(to_peer(up_z, src, dst, up_send.at[s - 1, h], up_recv.at[s - 1, h]))
        if s < half or h % 2 == 1:
            src, dst = place_down
            copies.append(to_peer(down_z, src, dst, down_send.at[s - 1, h], down_recv.at[s - 1, h]))
        return copies

    kv_pieces, weight_pieces = kr_send.shape[1], wr_send.shape[1]

    def kv_step(s, h):
        a, b = lax.rem(z + n + 1 - s, n), lax.rem(z + s - 1, n)
        size = tokens // kv_pieces
        one, two = kv.at[a, pl.ds(h * size, size)], kv.at[b, pl.ds(h * size, size)]
        return ring_pieces(s, h, (one, one), (two, two), (kr_send, kr_recv, kl_send, kl_recv))

    def weight_step(s, h):
        a, b = lax.rem(z + n + 1 - s, n), lax.rem(z + s - 1, n)
        size = chunk // weight_pieces
        window = pl.ds(h * size, size)
        one, two = weight.at[a, core, window], weight.at[b, core, window]
        own = weight_any.at[window, lanes(x * wide + core * chunk, chunk)]
        return ring_pieces(
            s,
            h,
            (own if s == 1 else one, one),
            (own if s == 1 else two, two),
            (wr_send, wr_recv, wl_send, wl_recv),
        )

    def share(off, h, side):
        k = lax.rem(z + off, n)
        size = chunk // weight_pieces
        block = weight.at[k, side, pl.ds(h * size, size)]
        return to_peer(sibling, block, block, sib_send.at[off, h], sib_recv.at[off, h])

    def weight_arrived(s, h):
        for copy in weight_step(s, h):
            copy.wait_recv()
        if s < half:
            for copy in weight_step(s + 1, h):
                copy.start()
            share(n - s, h, core).start()
        share(s, h, core).start()

    small = []
    for d in range(1, cols):
        for at, (src, dst) in enumerate(
            (
                (ids.at[x], ids.at[x]),
                (gates.at[x], gates.at[x]),
                (hidden_any.at[:, lanes(col[d] * wide, wide)], hidden.at[x]),
            )
        ):
            small.append(
                to_peer(same[d], src, dst, small_send.at[d, at], small_recv.at[cols - d, at])
            )
    for h in range(kv_pieces):
        for copy in kv_step(1, h):
            copy.start()
    for copy in small + expert_loads:
        copy.start()

    row = lax.broadcasted_iota(I32, (tokens, n * tokens), 0) + z * tokens
    column = lax.broadcasted_iota(I32, (tokens, n * tokens), 1)
    bias[...] = jnp.where(row >= column, 0.0, -1e30)

    acc[...] = jnp.zeros_like(acc)
    for s in range(1, half + 1):
        for h in range(kv_pieces):
            for copy in kv_step(s, h):
                copy.wait_recv()
            if s < half:
                for copy in kv_step(s + 1, h):
                    copy.start()
        for at, h in ((1,0),(2,1),(3,2),(3,3)):
            if s == at:
                for copy in weight_step(1, h):
                    copy.start()
    loads[4].wait()

    def place(j):
        odd = lax.rem(j, 2)
        off = odd * ((j + 1) // 2) + (1 - odd) * lax.rem(n - j // 2, n)
        return off, lax.rem(z + off, n)

    def chunk_first(j):
        _, k = place(j)
        return (
            to_peer(same[1], mixed.at[k, x], mixed.at[k, x], x_send.at[j, 0], x_recv.at[j, 0]),
            to_peer(same[cols - 1], mixed.at[k, x], mixed.at[k, x], x_send.at[j, 1], x_recv.at[j, 1]),
        )

    def chunk_second(j):
        _, k = place(j)
        cut = tokens // 2
        one = mixed.at[k, col[cols - 1], pl.ds(0, cut)]
        two = mixed.at[k, col[1], pl.ds(cut, cut)]
        return (
            to_peer(same[1], one, one, x_send.at[j, 2], x_recv.at[j, 2]),
            to_peer(same[cols - 1], two, two, x_send.at[j, 3], x_recv.at[j, 3]),
        )

    def chunk_forward(j):
        for copy in chunk_first(j):
            copy.wait_recv()
        for copy in chunk_second(j):
            copy.start()

    def project(j):
        off, k = place(j)
        for copy in chunk_second(j):
            copy.wait_recv()

        @pl.when(off > 0)
        def _():
            for h in range(weight_pieces):
                share(off, h, 1 - core).wait_recv()

        left = mixed[k].reshape(cols * tokens, chunk)
        for side in range(CORES):
            residual[:, side * chunk : (side + 1) * chunk] += jnp.dot(
                left, weight[k, side], preferred_element_type=F32
            )

    def places():
        expert = lax.broadcasted_iota(I32, (experts, tokens), 0)
        earlier = lax.broadcasted_iota(I32, (tokens, tokens), 0) < lax.broadcasted_iota(
            I32, (tokens, tokens), 1
        )
        earlier = jnp.where(earlier, 1.0, 0.0).astype(BF16)
        placed = []
        for q in range(cols):
            chosen = ids[q]
            named = jnp.where(expert == chosen, 1.0, 0.0)
            ahead = jnp.dot(named.astype(BF16), earlier, preferred_element_type=F32)
            rank = jnp.sum(ahead * named, axis=0, keepdims=True)
            placed.append(
                (chosen[0:1] * (cols * capacity) + q * capacity).astype(F32) + rank
            )
        return jnp.concatenate(placed, axis=1)

    scale = math.log2(math.e) / math.sqrt(HEAD_SIZE)

    @pl.loop(0, n)
    def _(j):
        _, k = place(j)
        kv_head = k // group
        key = kv[:, :, lanes(kv_head * HEAD_SIZE, HEAD_SIZE)].reshape(n * tokens, HEAD_SIZE)
        value = kv[
            :, :, lanes((KEY_VALUE_HEADS + kv_head) * HEAD_SIZE, HEAD_SIZE)
        ].reshape(n * tokens, HEAD_SIZE)
        for h in range(heads):
            scores = across(query[:, lanes(k * chunk + h * HEAD_SIZE, HEAD_SIZE)], key) + bias[...]
            top = jnp.max(scores, axis=-1, keepdims=True)
            shifted = jnp.exp2((scores - top) * scale)
            total = jnp.sum(shifted, axis=-1, keepdims=True)
            attended = jnp.dot(shifted.astype(BF16), value, preferred_element_type=F32)
            mixed[k, x, :, h * HEAD_SIZE : (h + 1) * HEAD_SIZE] = (attended / total).astype(BF16)
        for copy in chunk_first(j):
            copy.start()

        @pl.when(j == 1)
        def _():
            for copy in small:
                copy.wait_recv()
            loads[2].wait()
            loads[5].wait()
            residual[...] = hidden[...].reshape(cols * tokens, wide).astype(F32)

        @pl.when(j == 2)
        def _():
            slot = lax.broadcasted_iota(I32, selector.shape, 0).astype(F32)
            selector[...] = jnp.where(slot == places(), 1.0, 0.0).astype(BF16)

        @pl.when(j >= 1)
        def _():
            chunk_forward(j - 1)

        @pl.when(j == 1)
        def _():
            loads[0].wait()
            loads[1].wait()

        for at, (s, h) in ((0, (1, 0)), (1, (1, 1)), (1, (1, 2)), (2, (1, 3)), (3, (2, 0)), (3, (2, 1)), (4, (2, 2)), (5, (2, 3)), (6, (3, 0)), (6, (3, 1)), (7, (3, 2)), (7, (3, 3))):

            @pl.when(j == at)
            def _():
                weight_arrived(s, h)

        @pl.when(j >= 3)
        def _():
            project(j - 3)

    downs = []
    for d in (4, 3, 5, 2, 6, 1, 7):
        peer = lax.rem(z + d, n)
        downs.append(
            to_peer(
                {"ctx": peer},
                down_any.at[:, lanes(peer * part, part)],
                down.at[n - d],
                wd_send.at[d],
                wd_recv.at[n - d],
            )
        )
        downs[-1].start()
    chunk_forward(n - 1)
    project(n - 3)
    project(n - 2)
    for h in range(weight_pieces):
        weight_arrived(half, h)
    project(n - 1)
    res = residual[...]
    squared = res[:, 0:128] * res[:, 0:128]
    for at in range(128, wide, 128):
        squared += res[:, at : at + 128] * res[:, at : at + 128]
    squares[x] = lax.dot_general(
        jnp.ones((8, 128), F32),
        squared,
        (((1,), (1,)), ((), ())),
        precision=lax.Precision.HIGHEST,
        preferred_element_type=F32,
    )
    sums = [
        to_peer(same[d], squares.at[x], squares.at[x], sq_send.at[d], sq_recv.at[cols - d])
        for d in range(1, cols)
    ]
    for copy in sums:
        copy.start()
    for copy in sums:
        copy.wait_recv()
    total = squares[0]
    for q in range(1, cols):
        total += squares[q]
    inverse = jnp.transpose(lax.rsqrt(total * (1.0 / width) + 1e-06))[:, 0:1]

    def rows_place(h):
        return rows.at[0, h, pl.ds(pl.multiple_of(core * block_rows, 16), block_rows), lanes(x * stream, stream)]

    def dispatch(h):
        columns = residual[:, h * stream : (h + 1) * stream]
        gains = gain[:, lanes(x * wide + h * stream, stream)].astype(F32)
        normed = (columns * inverse * gains).astype(BF16)
        picked = jnp.dot(selector[...], normed, preferred_element_type=F32).astype(BF16)
        outgoing[h] = picked.reshape(experts, block_rows, stream)
        copies = []
        for d in (4, 5, 2, 6, 3, 7, 1):
            e = lax.rem(me + d, experts)
            copies.append(
                to_peer(
                    {"exp": e},
                    outgoing.at[h, e],
                    rows_place(h),
                    disp_send.at[d, h],
                    disp_recv.at[experts - d, h],
                )
            )
            copies[-1].start()
        keep = pltpu.make_async_copy(outgoing.at[h, me], rows_place(h), disp_recv.at[0, h])
        keep.start()
        return copies, keep

    def rows_step(s, h):
        copies = []
        if s < half or h % 2 == 0:
            src, dst = rows.at[(n + 1 - s) % n, h], rows.at[n - s, h]
            copies.append(to_peer(up_z, src, dst, rr_send.at[s - 1, h], rr_recv.at[s - 1, h]))
        if s < half or h % 2 == 1:
            src, dst = rows.at[s - 1, h], rows.at[s, h]
            copies.append(to_peer(down_z, src, dst, rl_send.at[s - 1, h], rl_recv.at[s - 1, h]))
        return copies

    order = [0, 1, 7, 2, 6, 3, 5, 4]
    ready = [order.index(r) for r in range(n)]
    bounds = ((0, 3), (3, 7), (7, 8))

    def hid_step(part_at, s):
        first, end = bounds[part_at]
        blocks = pl.ds(first, end - first)
        one, here = hid.at[(n + 1 - s) % n, blocks], hid.at[n - s, blocks]
        two, there = hid.at[s - 1, blocks], hid.at[s, blocks]
        if s == half:
            cut = 128
            one, here = one.at[:, pl.ds(0, cut)], here.at[:, pl.ds(0, cut)]
            two, there = two.at[:, pl.ds(cut, count + pair - cut)], there.at[:, pl.ds(cut, count + pair - cut)]
        return (
            to_peer(up_z, one, here, hr_send.at[part_at, s - 1], hr_recv.at[part_at, s - 1]),
            to_peer(down_z, two, there, hl_send.at[part_at, s - 1], hl_recv.at[part_at, s - 1]),
        )

    def hid_start(part_at, s):
        copies = hid_step(part_at, s)
        for copy in copies:
            copy.start()
        sent.extend(copies)
        hid_now[part_at] = copies

    def hid_arrived(part_at, s):
        for copy in hid_now[part_at]:
            copy.wait_recv()
        if s < half:
            hid_start(part_at, s + 1)

    def unpack(r, p):
        packed = hid[r, p]
        end = packed[count : count + pair]
        rest = jnp.concatenate([end[:, 0 : units - 128], end[:, units - 128 :]], axis=0)
        return jnp.concatenate([packed[0:count], rest], axis=1)

    def shrink(part_at, *shards):
        @pl.loop(*bounds[part_at])
        def _(p):
            off, _ = place(p)
            for r in shards:
                acc[lax.rem(z + r + off, n)] += jnp.dot(
                    unpack(r, p), down[r], preferred_element_type=F32
                )

    def expand(r):
        gate_part, up_part = 0.0, 0.0
        for h in range(streams):
            block = rows[r, h]
            gate_part += across(block, gate[h])
            up_part += across(block, up[h])
        shown = (gate_part / (1.0 + jnp.exp(-gate_part)) * up_part).astype(BF16)
        hid[0, ready[r], 0:count, :] = shown[:, 0:128]
        hid[0, ready[r], count : count + pair, :] = jnp.concatenate(
            [shown[0:pair, 128:units], shown[pair:count, 128:units]], axis=1
        )

    dispatched = [dispatch(h) for h in range(streams)]
    sent = []
    steps = {}
    for h in range(streams):
        copies, keep = dispatched[h]
        sent += copies
        for copy in copies:
            copy.wait_recv()
        keep.wait()
        steps[1, h] = rows_step(1, h)
        for copy in steps[1, h]:
            copy.start()
        sent += steps[1, h]
    for copy in expert_loads:
        copy.wait()
    expand(0)
    placed_t = jnp.transpose(jnp.broadcast_to(places(), (8, cols * tokens)))[:, 0:1]
    slot = lax.broadcasted_iota(I32, selector_t.shape, 1).astype(F32)
    selector_t[...] = jnp.where(slot == placed_t, 1.0, 0.0).astype(BF16)
    hid_now = {}
    for s in range(1, half + 1):
        for h in range(streams):
            for copy in steps[s, h]:
                copy.wait_recv()
            if s < half:
                steps[s + 1, h] = rows_step(s + 1, h)
                for copy in steps[s + 1, h]:
                    copy.start()
                sent += steps[s + 1, h]
        if s > 1:
            hid_arrived(0, s - 1)
        if s < half:
            expand(s)
            expand(n - s)
        else:
            expand(half)
        if s == 1:
            hid_start(0, 1)
            loads[3].wait()
            for copy in downs:
                copy.wait_recv()
            shrink(0, 0)
        elif s == 2:
            shrink(0, 1, n - 1)
        elif s == 3:
            hid_start(1, 1)
            shrink(0, 2, n - 2)
            shrink(1, 0)
    hid_start(2, 1)
    hid_arrived(1, 1)
    shrink(0, 3, n - 3)
    shrink(1, 1, n - 1)
    hid_arrived(2, 1)
    shrink(2, 0, 1, n - 1)
    hid_arrived(1, 2)
    hid_arrived(2, 2)
    shrink(1, 2, n - 2)
    shrink(2, 2, n - 2)
    hid_arrived(1, 3)
    hid_arrived(2, 3)
    shrink(1, 3, n - 3)
    shrink(2, 3, n - 3)
    for part_at in range(len(bounds)):
        hid_arrived(part_at, half)

    def leave(d, i):
        b = lax.rem(z + d, n)
        window = lanes(i * piece, piece)
        return to_peer(
            {"ctx": b},
            obuf.at[d, :, window],
            out.at[z, :, window],
            out_send.at[d, i],
            out_recv.at[n - d, i],
        )

    def finish(i):
        window = lanes(i * piece, piece)
        for d in (4, 3, 5, 2, 6, 1, 7, 0):
            b = lax.rem(z + d, n)
            block = acc[b, :, window] + jnp.dot(
                unpack(half, ready[(d + half) % n]), down[half, :, window], preferred_element_type=F32
            )
            if d == 0:
                out[z, :, window] = block.astype(BF16)
            else:
                obuf[d, :, window] = block.astype(BF16)
                leave(d, i).start()

    def hand_back(r, c, i):
        source = lax.rem(z + r, n)
        owner = source // per_col * CORES + c
        side = lax.rem(source, per_col)
        rel = lax.rem(me - owner + experts, experts)
        src = out.at[source, pl.ds(c * block_rows, block_rows), lanes(i * piece, piece)]
        dst = back.at[me, :, lanes(side * part + i * piece, piece)]
        there = to_peer({"exp": owner}, src, dst, back_send.at[r, c, i], back_recv.at[rel, side, i])
        return owner, there, (src, dst, back_recv.at[0, side, i])

    def forward(i):
        for r in (0, 7, 1, 6, 2, 5, 3, 4):
            if r > 0:
                source = lax.rem(z + r, n)
                landed = out.at[source, :, lanes(i * piece, piece)]
                pltpu.make_async_copy(landed, landed, out_recv.at[r, i]).wait()
            for c in range(CORES):
                owner, there, here = hand_back(r, c, i)

                @pl.when(owner != me)
                def _():
                    there.start()

                @pl.when(owner == me)
                def _():
                    pltpu.make_async_copy(*here).start()

    def last(side, q, source, i):
        dst = result.at[:, lanes(source * wide + side * part + i * piece, piece)]
        return to_peer(
            {"section": after, "exp": q * CORES + core},
            stage.at[i, side, q],
            dst,
            last_send.at[i, side, q],
            last_recv.at[i, side, source],
        )

    gate_column = gates[...].reshape(cols * tokens, 128)[:, 0:1]

    def combine(i):
        for side in range(per_col):
            window = lanes(side * part + i * piece, piece)
            for e in range(experts):
                rel = lax.rem(e - me + experts, experts)
                landed = back.at[e, :, window]
                pltpu.make_async_copy(landed, landed, back_recv.at[rel, side, i]).wait()
            routed = jnp.dot(
                selector_t[...],
                back[:, :, window].reshape(experts * block_rows, piece),
                preferred_element_type=F32,
            )
            mixture = routed * gate_column + residual[:, window]
            stage[i, side] = mixture.astype(BF16).reshape(cols, tokens, piece)
            for q in range(cols):
                last(side, q, x, i).start()

    @pl.loop(0, pieces + 2)
    def _(t):
        @pl.when(t < pieces)
        def _():
            finish(t)

        @pl.when((t >= 1) & (t < pieces + 1))
        def _():
            forward(t - 1)

        @pl.when(t >= 2)
        def _():
            combine(t - 2)

    @pl.loop(0, pieces)
    def _(i):
        for side in range(per_col):
            for q in range(cols):
                last(side, q, q, i).wait_recv()
                last(side, q, x, i).wait_send()
        for r in range(n):
            if r > 0:
                leave(r, i).wait_send()
            for c in range(CORES):
                owner, there, _ = hand_back(r, c, i)

                @pl.when(owner != me)
                def _():
                    there.wait_send()

    for copy in small + sums + sent + downs:
        copy.wait_send()
    for s in range(1, half + 1):
        for h in range(kv_pieces):
            for copy in kv_step(s, h):
                copy.wait_send()
        for h in range(weight_pieces):
            for copy in weight_step(s, h):
                copy.wait_send()
    for off in range(1, n):
        for h in range(weight_pieces):
            share(off, h, core).wait_send()

    @pl.loop(0, n)
    def _(j):
        for copy in chunk_first(j) + chunk_second(j):
            copy.wait_send()


def run_layer(query, key, value, ids, gates, gain, hidden, weight, gate, up, down):
    n = lax.axis_size("ctx")
    experts = lax.axis_size("exp")
    sections = lax.axis_size("section")
    cols = experts // CORES
    tokens, width = query.shape
    wide, part = width // cols, width // n
    units = down.shape[0]
    capacity = 5 * tokens // (4 * experts)
    count = experts * capacity
    packed = count + count // 2
    streams = 2
    pieces = part // 128
    dma = pltpu.SemaphoreType.DMA
    anywhere = pl.BlockSpec(memory_space=pl.ANY)
    return pl.pallas_call(
        functools.partial(layer_kernel, n, cols, sections, capacity),
        out_shape=jax.ShapeDtypeStruct((tokens, width), BF16),
        in_specs=[anywhere] * 11,
        out_specs=anywhere,
        scratch_shapes=[
            pltpu.VMEM((tokens, width), BF16),
            pltpu.VMEM(ids.shape, I32),
            pltpu.VMEM(gates.shape, F32),
            pltpu.VMEM(gain.shape, BF16),
            pltpu.VMEM((n, tokens, 2 * key.shape[1]), BF16),
            pltpu.VMEM((n, cols, tokens, part), BF16),
            pltpu.VMEM((n, CORES, part, part), BF16),
            pltpu.VMEM((cols, tokens, wide), BF16),
            pltpu.VMEM((cols, experts, tokens), I32),
            pltpu.VMEM((cols, tokens, 128), F32),
            pltpu.VMEM((cols, 8, cols * tokens), F32),
            pltpu.VMEM((tokens, n * tokens), F32),
            pltpu.VMEM((cols * tokens, wide), F32),
            pltpu.VMEM((experts * cols * capacity, cols * tokens), BF16),
            pltpu.VMEM((cols * tokens, experts * cols * capacity), BF16),
            pltpu.VMEM((streams, experts, count // CORES, wide // streams), BF16),
            pltpu.VMEM((n, streams, count, width // streams), BF16),
            pltpu.VMEM((streams, units, width // streams), BF16),
            pltpu.VMEM((streams, units, width // streams), BF16),
            pltpu.VMEM((n, units, part), BF16),
            pltpu.VMEM((n, n, packed, 128), BF16),
            pltpu.VMEM((n, count, part), F32),
            pltpu.VMEM((n, count, part), BF16),
            pltpu.VMEM((n, count, part), BF16),
            pltpu.VMEM((experts, count // CORES, wide), BF16),
            pltpu.VMEM((pieces, wide // part, cols, tokens, 128), BF16),
            dma((10,)),
            dma((streams, cols)),
            dma((streams, cols)),
        ]
        + [dma((n // 2, 2))] * 4
        + [dma((n // 2, 4))] * 4
        + [dma((n, 4))] * 2
        + [dma((n, 4))] * 2
        + [dma((cols, 3))] * 2
        + [dma((cols,))] * 2
        + [dma((n,))] * 2
        + [dma((experts, streams))] * 2
        + [dma((n // 2, streams))] * 4
        + [dma((3, n // 2))] * 4
        + [dma((n, pieces))] * 2
        + [dma((n, CORES, pieces)), dma((experts, wide // part, pieces))]
        + [dma((pieces, wide // part, cols))] * 2,
        compiler_params=pltpu.CompilerParams(
            collective_id=0, has_side_effects=True, vmem_limit_bytes=60 * 2**20
        ),
        cost_estimate=pl.CostEstimate(
            flops=2 * cols * tokens * width * wide + 6 * n * count * width * units,
            bytes_accessed=16 * 2**20,
            transcendentals=QUERY_HEADS * tokens * n * tokens,
        ),
    )(query, key, value, ids, gates, gain, hidden, weight, gate, up, down)


def per_device(
    hidden_in,
    queries,
    keys,
    values,
    out_weight,
    norm_gain,
    w_gate,
    w_up,
    w_down_t,
    expert_ids,
    route_gates,
):
    tokens_here = hidden_in.shape[2]
    moved = run_layer(
        queries[0, 0],
        keys[0, 0],
        values[0, 0],
        expert_ids[0, 0].reshape(1, tokens_here),
        route_gates[0, 0].reshape(1, tokens_here),
        norm_gain,
        hidden_in[0, 0],
        out_weight[0],
        w_gate[0, 0].T,
        w_up[0, 0].T,
        w_down_t[0, 0].T,
    )
    return moved.reshape(1, 1, tokens_here, D)


def solution(mesh):
    return jax.shard_map(
        per_device,
        mesh=mesh,
        in_specs=(
            P("section", "exp", "ctx", None),
            P("section", "exp", "ctx", None),
            P("section", "exp", "ctx", None),
            P("section", "exp", "ctx", None),
            P("section", "ctx", None),
            P("section", None),
            P("section", "exp", None, "ctx"),
            P("section", "exp", None, "ctx"),
            P("section", "exp", None, "ctx"),
            P("section", "exp", "ctx", None),
            P("section", "exp", "ctx", None),
        ),
        out_specs=P("section", "exp", "ctx", None),
        check_vma=False,
    )
```
